256 devices in a mesh: list: 64 (over x, z, core), row: 4 (over y).
Axes of the slice: x: 4, y: 4, z: 8, core: 2. Of those that a mesh axis runs over, the one named last changes fastest.
Arguments:
- queries: bfloat16 [16384, 256], P('list'), may hold values from -6 to 6
- query_owner: int32 [16384], P('list'), may hold values from 0 to 7
- probes: int32 [16384, 4], P('list'), may hold values from 0 to 127, all different within a row; in each aligned block of 256 rows (0 to 255, 256 to 511, ...) at most 16 rows name the same one
- list_slab: bfloat16 [128, 16384, 256], P('list', 'row'), may hold values from -48 to 48
- row_owner: int32 [128, 16384], P('list', 'row'), may hold values from 0 to 7
- proj_in: bfloat16 [512, 1024], P(None, 'row'), may hold values from -0.25 to 0.25
- bias_in: bfloat16 [1024], P('row'), may hold values from -4 to 4
- proj_out: bfloat16 [1024, 256], P('row'), may hold values from -0.1875 to 0.1875
Outputs:
- merged_out: bfloat16 [16384, 256], P('list', 'row')
The draws below stay inside these ranges and needn't reach their ends.
Inputs may be any that keep to these rules, and one draw needn't show every extreme that they name: Within the rows of one device's block of 256 queries, at most 16 probes name the same list, and that many in some blocks; the 4 probes of a query are distinct.
All inputs are finite; a program needn't handle non-finite values.
Results may differ from the reference program's by a relative error of at most 0.0055.
Values may be sent and summed in bfloat16 or wider, within the bound.
A program may use at most 128 MiB of HBM per device.

```python
import math
import jax
import jax.numpy as jnp
import numpy as np
from jax import lax

E = 256
FH = 1024
PROBES = 4
OWNERS = 8
Q_DEV = 256
NLIST = 128
ROWS = 16384
QUERIES = 16384
CAP = 16
N_LIST = 64


def draw_queries(key, part):
    inner_key = jax.random.fold_in(key, 21)
    key_base = jax.random.fold_in(inner_key, 0)
    values = jnp.clip(jax.random.normal(key_base, (QUERIES, E), jnp.float32), -4.0, 4.0) * 0.1
    return values.astype(jnp.bfloat16)


def draw_list_slab(key, part):
    inner_key = jax.random.fold_in(key, 31)
    key_base, key_rowscale, key_colscale = jax.random.split(inner_key, 3)
    row_scale = jnp.exp(jax.random.uniform(key_rowscale, (NLIST, ROWS, 1), jnp.float32, math.log(0.4), math.log(4.0)))
    col_scale = jnp.exp(jax.random.uniform(key_colscale, (1, 1, E), jnp.float32, math.log(0.3), math.log(3.0)))
    values = jnp.clip(jax.random.normal(key_base, (NLIST, ROWS, E), jnp.float32), -4.0, 4.0) * row_scale * col_scale
    return values.astype(jnp.bfloat16)


def with_ends(drawn, stream_key, low, high):
    longest = drawn.shape.index(max(drawn.shape))
    spots = []
    for shift in (0, 1):
        where = [jax.random.randint(jax.random.fold_in(stream_key, axis), (), 0, length) for axis, length in enumerate(drawn.shape)]
        where[longest] = (where[longest] + shift) % drawn.shape[longest]
        spots.append(tuple(where))
    return drawn.at[spots[0]].set(low).at[spots[1]].set(high)


def block_levels(own_key, dims, pieces, smallest, largest):
    factor_of, own = 1.0, jax.random.fold_in(own_key, 6)
    for dim, shards_of in pieces:
        heights = jnp.exp(jax.random.uniform(jax.random.fold_in(own, dim), (shards_of,), jnp.float32, smallest / len(pieces), largest / len(pieces)))
        factor_of = factor_of * jnp.repeat(heights, dims[dim] // shards_of).reshape([-1 if axis == dim else 1 for axis in range(len(dims))])
    return factor_of


def assign_block(rng, own, number, rows, number_of, top, bound, skew):
    order = jax.random.permutation(rng, number_of)
    crowded, ordinary = portions_of(number_of, rows * top, bound, skew, True), portions_of(number_of, rows * top, bound, skew, False)
    places = jnp.arange(number_of)

    def named(lengths, rotation):
        used = int((lengths > 0).sum())
        fixed = max(1, used // 4)
        moved = fixed + (places - fixed + rotation * (used - fixed)) % max(1, number_of - fixed)
        return jnp.zeros((number_of,), jnp.int32).at[order[jnp.where(places < fixed, places, moved)]].set(jnp.asarray(lengths, jnp.int32))

    lengths = jnp.where(number % 4 == 0, named(crowded, number // 4), named(ordinary, number - number // 4 - 1))
    mixed = jax.random.permutation(jax.random.fold_in(own, 3), number_of)
    source_of, sink = mixed[0:number_of // 2 * 2:2], mixed[1:number_of // 2 * 2:2]
    room = jnp.minimum(lengths[source_of] - 1, bound - lengths[sink]) // 2
    room = jnp.where((source_of == order[0]) | (sink == order[0]) | (lengths[sink] == 0), 0, jnp.maximum(room, 0))
    moved = jax.random.randint(jax.random.fold_in(own, 4), (number_of // 2,), 0, 1 << 20) % (room + 1)
    lengths = lengths.at[source_of].add(-moved).at[sink].add(moved)
    labels = jnp.searchsorted(jnp.cumsum(lengths), jnp.arange(rows * top), side="right").astype(jnp.int32)
    table = labels.reshape(top, rows).T
    table = table[jax.random.permutation(jax.random.fold_in(own, 1), rows)]
    rotation = jax.random.randint(jax.random.fold_in(own, 2), (rows, 1), 0, top)
    return jnp.take_along_axis(table, (jnp.arange(top)[None, :] + rotation) % top, axis=1)


def portions_of(number_of, total, most, slope, full):
    weights = [(1 << 20) // math.isqrt(rank ** slope) + 1 for rank in range(1, number_of + 1)]
    largest = most if full else min(most, max(-(-total // number_of), total * weights[0] // sum(weights)))
    least = 1 if total - largest >= number_of - 1 else 0
    counts, rest = [largest] + [least] * (number_of - 1), total - largest - least * (number_of - 1)
    while rest > 0:
        free = [i for i in range(1, number_of) if counts[i] < largest] or [i for i in range(1, number_of) if counts[i] < most]
        whole, budget = sum([weights[i] for i in free]), rest
        for i in free:
            addition = min(most - counts[i], max(1, budget * weights[i] // whole), rest)
            counts[i] = counts[i] + addition
            rest = rest - addition
    return np.array(counts)


def gaussian(rng, dims, spread, most, cuts=(), held_as=jnp.bfloat16):
    level = block_levels(rng, dims, cuts, -0.22, 0.18) if cuts else 1.0
    array = jax.random.normal(rng, dims, jnp.float32) * spread * level
    return jnp.minimum(jnp.maximum(array, -most), most).astype(held_as)


def setup_inputs(seed: int = 0) -> dict:
    splits = jax.random.split(jax.random.key(seed), 9)
    queries = draw_queries(jax.random.fold_in(splits[8], 71), 0)
    query_owner = with_ends(jax.random.randint(splits[1], (QUERIES,), 0, OWNERS), jax.random.fold_in(splits[1], 1), 0, OWNERS - 1).astype(jnp.int32)
    probes_keys = jax.random.split(jax.random.fold_in(splits[2], 1), QUERIES // Q_DEV)
    probes_turns = jax.random.permutation(jax.random.fold_in(splits[2], 3), QUERIES // Q_DEV)
    probes = jax.vmap(lambda own, number: assign_block(jax.random.fold_in(splits[2], 2), own, number, Q_DEV, NLIST, PROBES, CAP, 2))(probes_keys, probes_turns).reshape((QUERIES, PROBES))
    list_slab = draw_list_slab(jax.random.fold_in(splits[8], 71), 0)
    row_owner = with_ends(jax.random.randint(splits[4], (NLIST, ROWS), 0, OWNERS), jax.random.fold_in(splits[4], 1), 0, OWNERS - 1).astype(jnp.int32)
    proj_in = gaussian(splits[5], (2 * E, FH), (2 * E) ** -0.5, 0.25, ((1, 4),))
    bias_in = gaussian(splits[6], (FH,), 1.0, 4.0, ((0, 4),))
    proj_out = gaussian(splits[7], (FH, E), FH ** -0.5, 0.1875, ((0, 4),))
    return {"queries": queries, "query_owner": query_owner, "probes": probes, "list_slab": list_slab, "row_owner": row_owner, "proj_in": proj_in, "bias_in": bias_in, "proj_out": proj_out}


SCORE_PEN = 10000.0

def reference(queries, query_owner, probes, list_slab, row_owner, proj_in, bias_in, proj_out):
    request_count = Q_DEV * PROBES
    per_block = probes.reshape(N_LIST, request_count).astype(jnp.int32)
    list_ids = jnp.arange(NLIST, dtype=jnp.int32)

    def ranks_of(probe_block):
        onehot = (probe_block[:, None] == list_ids[None, :]).astype(jnp.int32)
        before = jnp.cumsum(onehot, axis=0) - onehot
        return lax.optimization_barrier(jnp.sum(before * onehot, axis=1)).astype(jnp.int32)
    slot_rank = lax.map(ranks_of, per_block)
    source_ids = jnp.arange(N_LIST, dtype=jnp.int32)[:, None]
    request_ids = jnp.arange(request_count, dtype=jnp.int32)[None, :]
    position = (per_block * (N_LIST * CAP) + source_ids * CAP + slot_rank).astype(jnp.int32)
    query_ids = (source_ids * Q_DEV + request_ids // PROBES).astype(jnp.int32)
    slot_table = jnp.full((NLIST * N_LIST * CAP,), QUERIES, dtype=jnp.int32)
    slot_table = slot_table.at[position.reshape(-1)].set(query_ids.reshape(-1)).reshape(NLIST, N_LIST * CAP)
    padded_q = jnp.concatenate([queries, jnp.zeros((1, E), queries.dtype)], axis=0)
    padded_owner = jnp.concatenate([query_owner.astype(jnp.int32), jnp.full((1,), -1, dtype=jnp.int32)])
    score_scale = 1.0 / math.sqrt(E)

    def one_list(packed):
        slot_ids, key_rows, owners = packed
        rows_q = padded_q[slot_ids]
        score = jnp.dot(rows_q, key_rows.T, preferred_element_type=jnp.float32) * score_scale
        same = (padded_owner[slot_ids][:, None] == owners[None, :]).astype(jnp.float32)
        score = score - SCORE_PEN * same
        peak = lax.optimization_barrier(jnp.max(score, axis=1, keepdims=True))
        weight = jnp.exp(score - peak)
        total = lax.optimization_barrier(jnp.sum(weight, axis=1, keepdims=True))
        weighted = jnp.dot(weight.astype(jnp.bfloat16), key_rows, preferred_element_type=jnp.float32)
        return (weighted / total).astype(jnp.bfloat16)
    contexts = lax.map(one_list, (slot_table, list_slab, row_owner))
    flat_ctx = contexts.reshape(NLIST * N_LIST * CAP, E)
    picked = flat_ctx[position.reshape(-1)].astype(jnp.float32).reshape(QUERIES, PROBES, E)
    retrieved = lax.optimization_barrier(jnp.mean(picked, axis=1))
    normed = retrieved * lax.rsqrt(lax.optimization_barrier(jnp.mean(retrieved * retrieved, axis=1, keepdims=True)) + 1e-06)
    joined = jnp.concatenate([queries.astype(jnp.float32), normed], axis=1).astype(jnp.bfloat16)
    hidden = jnp.dot(joined, proj_in, preferred_element_type=jnp.float32) + bias_in.astype(jnp.float32)
    hidden = jax.nn.gelu(hidden, approximate=True).astype(jnp.bfloat16)
    return jnp.dot(hidden, proj_out, preferred_element_type=jnp.float32).astype(jnp.bfloat16)
```

```python
import math

import jax
import jax.numpy as jnp
from jax import lax
from jax.experimental import pallas as pl
from jax.experimental.pallas import tpu as pltpu
from jax.sharding import PartitionSpec as P

SCORE_PEN = 10000.0
LOG2E = math.log2(math.e)
NX, NZ, NC, NY = 4, 8, 2, 4
CAP = 16
TILE = 512
MESH = pl.DeviceIdType.MESH
F32 = jnp.float32
BF16 = jnp.bfloat16


def xor(a, b, bits):
    out = 0
    for i in range(bits):
        out = out + ((a // 2**i + b // 2**i) % 2) * 2**i
    return out


def nt_dot(a, b):
    return lax.dot_general(a, b, (((1,), (1,)), ((), ())), preferred_element_type=F32)


def kernel(
    q_ref, owner_ref, probes_ref, slab_hbm, rowner_ref, win_ref, bias_ref, wout_ref,
    out_ref,
    slab, kt, rcol, onehot, onehot_t, send_q, send_o, recv_q, recv_o, own_o, qt, scores, acc,
    part, lse, rpart, rlse, ctx, ret, pq, rpq, blk, rblk, wi, wo, bi,
    slab_sem, a2a_s, a2a_r, o_s, o_r, ag_s, ag_r, ago_s, ago_r, w_s, w_r, rs_s, rs_r, rl_s, rl_r,
    ret_s, ret_r, pq_s, pq_r, blk_s, blk_r, loc_sem,
):
    nk = NZ * NC
    nq = nk * CAP
    rows = slab.shape[1]
    feat = slab.shape[2]
    tile = scores.shape[2]
    ntile = rows // tile
    li = lax.axis_index("list")
    y = lax.axis_index("row")
    core = li % NC
    z = (li // NC) % NZ
    x = li // (NC * NZ)

    def partner(k):
        dz, dc = k // NC, k % NC
        return (xor(x, xor(y, dz % 4, 2), 2) * NZ + xor(z, dz, 3)) * NC + (core + dc) % NC

    def peer(j):
        return (y + j) % NY

    barrier = pltpu.get_barrier_semaphore()
    for j in (1, 2, 3):
        pl.semaphore_signal(barrier, inc=1, device_id=(li, peer(j)), device_id_type=MESH)

    @pl.when(y != 0)
    def _():
        pl.semaphore_signal(barrier, inc=1, device_id=(partner(0), y), device_id_type=MESH)

    def sig(k, c):
        pl.semaphore_signal(barrier, inc=1, device_id=(partner(k), y), device_id_type=MESH)
        return c

    lax.fori_loop(1, nk, sig, 0)

    slab_copies = [pltpu.make_async_copy(slab_hbm.at[l], slab.at[l], slab_sem.at[l]) for l in range(2)]
    for c in slab_copies:
        c.start()

    nl = 2 * nk
    row = lax.broadcasted_iota(jnp.int32, (nl, q_ref.shape[0]), 0)
    kk = row // 2
    dz = kk // NC
    xd = x ^ y ^ (dz & 3)
    zd = z ^ dz
    cd = (core + kk) % NC
    lvec = ((xd * NZ + zd) * NC + cd) * 2 + row % 2
    hit = probes_ref[0:1, :] == lvec
    for j in range(1, 4):
        hit = hit | (probes_ref[j : j + 1, :] == lvec)
    hits = jnp.where(hit, 1.0, 0.0).astype(F32)
    qn = q_ref.shape[0]
    before = jnp.where(
        lax.broadcasted_iota(jnp.int32, (qn, qn), 0) < lax.broadcasted_iota(jnp.int32, (qn, qn), 1), 1.0, 0.0
    ).astype(BF16)
    rank = jnp.dot(hits.astype(BF16), before, preferred_element_type=F32)
    rank = jnp.where(hit, rank, -1.0)
    slot = lax.broadcasted_iota(jnp.int32, (CAP, qn), 0).astype(F32)
    for r in range(nl):
        onehot[r // 2, r % 2] = jnp.where(rank[r : r + 1, :] == slot, 1.0, 0.0).astype(BF16)
    oh = onehot[...].reshape(nl * CAP, qn)
    picked = jnp.dot(oh, q_ref[...], preferred_element_type=F32) * (1.0 / math.sqrt(feat))
    send_q[...] = picked.astype(BF16).reshape(send_q.shape)
    own8 = jnp.broadcast_to((owner_ref[...] + 1).astype(F32), (8, qn)).astype(BF16)
    for i in range(2):
        send_o[i : i + 1, :] = nt_dot(own8, onehot[:, i].reshape(nq, qn))[0:1, :]
    bi[y] = jnp.broadcast_to(bias_ref[...].astype(F32), (8, bias_ref.shape[1]))

    pl.semaphore_wait(barrier, 19 - 16 + nk - (1 - (y + 3) // 4))

    def q_copy(k):
        return pltpu.make_async_remote_copy(
            src_ref=send_q.at[k], dst_ref=recv_q.at[y, k], send_sem=a2a_s.at[k], recv_sem=a2a_r.at[k],
            device_id=(partner(k), y), device_id_type=MESH)

    def o_copy(k):
        return pltpu.make_async_remote_copy(
            src_ref=send_o, dst_ref=recv_o.at[k], send_sem=o_s.at[k], recv_sem=o_r.at[k],
            device_id=(partner(k), y), device_id_type=MESH)

    q_self = pltpu.make_async_copy(send_q.at[0], recv_q.at[y, 0], a2a_r.at[0])
    o_self = pltpu.make_async_copy(send_o, recv_o.at[0], o_r.at[0])

    @pl.when(y == 0)
    def _():
        q_self.start()
        o_self.start()

    @pl.when(y != 0)
    def _():
        q_copy(0).start()
        o_copy(0).start()

    def a2a_start(k, c):
        q_copy(k).start()
        o_copy(k).start()
        return c

    lax.fori_loop(1, nk, a2a_start, 0)

    def w_copies(j):
        dev = (li, peer(j))
        return [
            pltpu.make_async_remote_copy(
                src_ref=s, dst_ref=d.at[y], send_sem=w_s.at[n, j - 1], recv_sem=w_r.at[n, j - 1],
                device_id=dev, device_id_type=MESH)
            for n, (s, d) in enumerate(((win_ref, wi), (wout_ref, wo), (bi.at[y], bi)))
        ]

    weight_copies = [c for j in (1, 2, 3) for c in w_copies(j)]
    for c in weight_copies:
        c.start()
    local = [pltpu.make_async_copy(win_ref, wi.at[y], loc_sem.at[0]), pltpu.make_async_copy(wout_ref, wo.at[y], loc_sem.at[1])]
    for c in local:
        c.start()

    onehot_t[...] = oh.astype(F32).T.astype(BF16)
    for l in range(2):
        slab_copies[l].wait()

        def prep(t, c):
            blkk = slab[l, pl.ds(t * tile, tile), :]
            kt[l, t, 0:feat, :] = blkk.astype(F32).T.astype(BF16)
            kt[l, t, feat : feat + 16, :] = jnp.ones((16, tile), BF16)
            for h in range(tile // 128):
                rr = rowner_ref[l : l + 1, pl.ds(t * tile + h * 128, 128)].astype(F32)
                rcol[l, pl.ds(t * tile + h * 128, 128), :] = jnp.broadcast_to(rr, (128, 128)).T
            return c

        lax.fori_loop(0, ntile, prep, 0)

    @pl.when(y == 0)
    def _():
        q_self.wait()
        o_self.wait()

    @pl.when(y != 0)
    def _():
        q_copy(0).wait()
        o_copy(0).wait()

    def a2a_wait(k, c):
        q_copy(k).wait()
        o_copy(k).wait()
        return c

    lax.fori_loop(1, nk, a2a_wait, 0)
    lane_k = lax.broadcasted_iota(jnp.int32, (2, nq), 1) // CAP
    total_o = jnp.zeros((2, nq), F32)
    for k in range(nk):
        total_o = total_o + jnp.where(lane_k == k, recv_o[k], 0.0)
    own_o[y] = total_o - 1.0

    def ag_copies(j):
        dev = (li, peer(j))
        return [
            pltpu.make_async_remote_copy(
                src_ref=s.at[y], dst_ref=s.at[y], send_sem=ss.at[j - 1], recv_sem=rr.at[j - 1],
                device_id=dev, device_id_type=MESH)
            for s, ss, rr in ((recv_q, ag_s, ag_r), (own_o, ago_s, ago_r))
        ]

    ag = {j: ag_copies(j) for j in (1, 3, 2)}
    for j in (1, 3, 2):
        for c in ag[j]:
            c.start()

    order = [(0, 0), (1, 0), (3, 0), (1, 1), (3, 1), (2, 0), (2, 1), (0, 1)]
    arrived = {0}
    rs_sends = []

    def rs_copies(j, l):
        dev = (li, peer(j))
        return [
            pltpu.make_async_remote_copy(
                src_ref=part.at[peer(j), l], dst_ref=rpart.at[j - 1, l], send_sem=rs_s.at[j - 1, l],
                recv_sem=rs_r.at[j - 1, l], device_id=dev, device_id_type=MESH),
            pltpu.make_async_remote_copy(
                src_ref=lse.at[peer(j), l], dst_ref=rlse.at[j - 1, l], send_sem=rl_s.at[j - 1, l],
                recv_sem=rl_r.at[j - 1, l], device_id=dev, device_id_type=MESH),
        ]

    def score_tile(n, l, t, own_row, m):
        s = jnp.dot(slab[l, pl.ds(t * tile, tile), :], qt[n % 2], preferred_element_type=F32)
        rc = rcol[l, pl.ds(t * tile, tile), :]
        halves = []
        for h in range(nq // 128):
            cols = slice(h * 128, (h + 1) * 128)
            sh = s[:, cols]
            sh = jnp.where(rc == own_row[:, cols], sh - SCORE_PEN, sh)
            scores[n % 2, t, :, cols] = sh
            halves.append(jnp.max(sh.reshape(tile // 8, 8, 128), axis=0))
        return jnp.maximum(m, jnp.concatenate(halves, axis=1))

    def sum_tile(n, l, t, peak):
        w = jnp.exp2(((scores[n % 2, t] - peak) * LOG2E).astype(BF16))
        acc[...] += jnp.dot(kt[l, t], w, preferred_element_type=F32)

    peak = None
    for n in range(len(order) + 1):
        own_row = None
        if n < len(order):
            j, l = order[n]
            src = peer(NY - j)
            if j not in arrived:
                for c in ag[j]:
                    c.wait_recv()
                arrived.add(j)
            src = peer(NY - j)
            qt[n % 2] = recv_q[src, :, l].reshape(nq, feat).astype(F32).T.astype(BF16)
            own_row = own_o[src, l : l + 1, :]
        if n > 0:
            acc[...] = jnp.zeros_like(acc)
        prev_peak = peak

        def stage(t, m, n=n, own_row=own_row, prev_peak=prev_peak):
            if n > 0:
                sum_tile(n - 1, order[n - 1][1], t, prev_peak)
            if n < len(order):
                m = score_tile(n, order[n][1], t, own_row, m)
            return m

        m = lax.fori_loop(0, ntile, stage, jnp.full((8, nq), -jnp.inf, F32))
        if n > 0:
            pj, pl_ = order[n - 1]
            psrc = peer(NY - pj)
            total = acc[feat : feat + 1, :]
            mean = acc[0:feat, :] / total
            part[psrc, pl_] = mean.T.astype(BF16)
            lse[psrc, pl_] = prev_peak + jnp.log(total)
            if pj != 0:
                for c in rs_copies(NY - pj, pl_):
                    c.start()
                    rs_sends.append(c)
        if n < len(order):
            peak = jnp.max(m, axis=0, keepdims=True)

    for l in range(2):
        for j in (1, 3, 2):
            for c in rs_copies(j, l):
                c.wait_recv()
        ls = [lse[y, l]] + [rlse[j - 1, l] for j in (1, 2, 3)]
        top = jnp.maximum(jnp.maximum(ls[0], ls[1]), jnp.maximum(ls[2], ls[3]))
        es = [jnp.exp(v - top) for v in ls]
        inv = 1.0 / (es[0] + es[1] + es[2] + es[3])
        cols = [jnp.broadcast_to(e * inv, (128, nq)).T for e in es]
        srcs = [part[y, l]] + [rpart[j - 1, l] for j in (1, 2, 3)]
        for h in range(feat // 128):
            cs = slice(h * 128, (h + 1) * 128)
            val = cols[0] * srcs[0][:, cs].astype(F32)
            for a in range(1, 4):
                val = val + cols[a] * srcs[a][:, cs].astype(F32)
            ctx[:, l, :, cs] = val.astype(BF16).reshape(nk, CAP, 128)

    def ret_copy(k):
        return pltpu.make_async_remote_copy(
            src_ref=ctx.at[k], dst_ref=ret.at[k], send_sem=ret_s.at[k], recv_sem=ret_r.at[k],
            device_id=(partner(k), y), device_id_type=MESH)

    ret_self = pltpu.make_async_copy(ctx.at[0], ret.at[0], ret_r.at[0])

    @pl.when(y == 0)
    def _():
        ret_self.start()

    @pl.when(y != 0)
    def _():
        ret_copy(0).start()

    def ret_start(k, c):
        ret_copy(k).start()
        return c

    lax.fori_loop(1, nk, ret_start, 0)

    @pl.when(y == 0)
    def _():
        ret_self.wait()

    @pl.when(y != 0)
    def _():
        ret_copy(0).wait()

    def ret_wait(k, c):
        ret_copy(k).wait()
        return c

    lax.fori_loop(1, nk, ret_wait, 0)

    share = jnp.dot(onehot_t[...], ret[...].reshape(nl * CAP, feat), preferred_element_type=F32) * 0.25
    qb = qn // NY
    pq[...] = share.astype(BF16).reshape(NY, qb, feat)
    pq_copies = {}
    for j in (1, 2, 3):
        pq_copies[j] = pltpu.make_async_remote_copy(
            src_ref=pq.at[peer(j)], dst_ref=rpq.at[j - 1], send_sem=pq_s.at[j - 1], recv_sem=pq_r.at[j - 1],
            device_id=(li, peer(j)), device_id_type=MESH)
        pq_copies[j].start()
    for c in weight_copies:
        c.wait()
    for c in local:
        c.wait()
    mine = q_ref[pl.ds(pl.multiple_of(y * qb, qb), qb), :]
    for j in (1, 2, 3):
        pq_copies[j].wait()
    retrieved = pq[y].astype(F32)
    for j in (1, 2, 3):
        retrieved = retrieved + rpq[j - 1].astype(F32)
    normed = retrieved * lax.rsqrt(jnp.mean(retrieved * retrieved, axis=1, keepdims=True) + 1e-06)
    normed = normed.astype(BF16)
    res = jnp.zeros((qb, feat), F32)
    for b in range(NY):
        hid = jnp.dot(mine, wi[b, 0:feat, :], preferred_element_type=F32)
        hid = hid + jnp.dot(normed, wi[b, feat : 2 * feat, :], preferred_element_type=F32)
        hid = jax.nn.gelu(hid + bi[b, 0:1, :], approximate=True).astype(BF16)
        res = res + jnp.dot(hid, wo[b], preferred_element_type=F32)
    ob = feat // NY
    for b in range(NY):
        blk[b, :, 0:ob] = res[:, b * ob : (b + 1) * ob].astype(BF16)
        blk[b, :, ob:128] = jnp.zeros((qb, 128 - ob), BF16)
    blk_copies = {}
    for j in (1, 2, 3):
        blk_copies[j] = pltpu.make_async_remote_copy(
            src_ref=blk.at[peer(j)], dst_ref=rblk.at[y], send_sem=blk_s.at[j - 1], recv_sem=blk_r.at[j - 1],
            device_id=(li, peer(j)), device_id_type=MESH)
        blk_copies[j].start()
    out_ref[pl.ds(pl.multiple_of(y * qb, qb), qb), :] = blk[y][:, 0:ob]
    for j in (1, 2, 3):
        for c in ag[j]:
            c.wait_send()
    for c in rs_sends:
        c.wait_send()
    for j in (1, 2, 3):
        blk_copies[j].wait()
        src = peer(NY - j)
        out_ref[pl.ds(pl.multiple_of(src * qb, qb), qb), :] = rblk[src][:, 0:ob]


def body(queries, query_owner, probes, list_slab, row_owner, proj_in, bias_in, proj_out):
    qn, feat = queries.shape
    lists, rows = list_slab.shape[0], list_slab.shape[1]
    nk = NZ * NC
    nq = nk * CAP
    nl = 2 * nk
    tile = min(TILE, rows)
    nt = rows // tile
    hid = proj_in.shape[1]
    qb = qn // NY
    vm = pltpu.VMEM
    dma = pltpu.SemaphoreType.DMA
    vspec = pl.BlockSpec(memory_space=pltpu.VMEM)
    return pl.pallas_call(
        kernel,
        out_shape=jax.ShapeDtypeStruct((qn, feat // NY), BF16),
        in_specs=[vspec, vspec, vspec, pl.BlockSpec(memory_space=pl.ANY), vspec, vspec, vspec, vspec],
        out_specs=vspec,
        scratch_shapes=[
            vm((lists, rows, feat), BF16),
            vm((lists, nt, feat + 16, tile), BF16),
            vm((lists, rows, 128), F32),
            vm((nk, 2, CAP, qn), BF16),
            vm((qn, nl * CAP), BF16),
            vm((nk, 2, CAP, feat), BF16),
            vm((2, nq), F32),
            vm((NY, nk, 2, CAP, feat), BF16),
            vm((nk, 2, nq), F32),
            vm((NY, 2, nq), F32),
            vm((2, feat, nq), BF16),
            vm((2, nt, tile, nq), F32),
            vm((feat + 16, nq), F32),
            vm((NY, 2, nq, feat), BF16),
            vm((NY, 2, 1, nq), F32),
            vm((NY - 1, 2, nq, feat), BF16),
            vm((NY - 1, 2, 1, nq), F32),
            vm((nk, 2, CAP, feat), BF16),
            vm((nk, 2, CAP, feat), BF16),
            vm((NY, qb, feat), BF16),
            vm((NY - 1, qb, feat), BF16),
            vm((NY, qb, 128), BF16),
            vm((NY, qb, 128), BF16),
            vm((NY, 2 * feat, hid), BF16),
            vm((NY, hid, feat), BF16),
            vm((NY, 8, hid), F32),
            dma((2,)),
            dma((nk,)), dma((nk,)), dma((nk,)), dma((nk,)),
            dma((3,)), dma((3,)), dma((3,)), dma((3,)),
            dma((3, 3)), dma((3, 3)),
            dma((3, 2)), dma((3, 2)), dma((3, 2)), dma((3, 2)),
            dma((nk,)), dma((nk,)),
            dma((3,)), dma((3,)), dma((3,)), dma((3,)),
            dma((2,)),
        ],
        compiler_params=pltpu.CompilerParams(
            collective_id=0, has_side_effects=True, vmem_limit_bytes=56 * 1024 * 1024
        ),
    )(queries, query_owner.reshape(1, qn), probes.T, list_slab, row_owner, proj_in, bias_in.reshape(1, hid), proj_out)


def solution(mesh):
    in_specs = (
        P("list", None),
        P("list"),
        P("list", None),
        P("list", "row", None),
        P("list", "row"),
        P(None, "row"),
        P("row"),
        P("row", None),
    )
    out_specs = P("list", "row")
    return jax.shard_map(body, mesh=mesh, in_specs=in_specs, out_specs=out_specs, check_vma=False)
```

```python
import math

import jax
import jax.numpy as jnp
from jax import lax
from jax.experimental import pallas as pl
from jax.experimental.pallas import tpu as pltpu
from jax.sharding import PartitionSpec as P

SCORE_PEN = 10000.0
LOG2E = math.log2(math.e)
NX, NZ, NC, NY = 4, 8, 2, 4
CAP = 16
TILE = 2048
MESH = pl.DeviceIdType.MESH
F32 = jnp.float32
BF16 = jnp.bfloat16


def xor(a, b, bits):
    out = 0
    for i in range(bits):
        out = out + ((a // 2**i + b // 2**i) % 2) * 2**i
    return out


def nt_dot(a, b):
    return lax.dot_general(a, b, (((1,), (1,)), ((), ())), preferred_element_type=F32)


def kernel(
    q_ref, owner_ref, probes_ref, slab_hbm, rowner_ref, win_ref, bias_ref, wout_ref,
    out_ref,
    slab, kt, rcol, onehot, onehot_t, send_q, send_o, recv_q, recv_o, own_o, qt, scores, acc,
    part, lse, rpart, rlse, ctx, ret, pq, rpq, blk, rblk, wi, wo, bi,
    slab_sem, a2a_s, a2a_r, o_s, o_r, ag_s, ag_r, ago_s, ago_r, w_s, w_r, rs_s, rs_r, rl_s, rl_r,
    f_s, f_r, ret_s, ret_r, pq_s, pq_r, blk_s, blk_r, loc_sem,
):
    nk = NZ * NC
    nq = nk * CAP
    rows = slab.shape[1]
    feat = slab.shape[2]
    tile = scores.shape[2]
    ntile = rows // tile
    li = lax.axis_index("list")
    y = lax.axis_index("row")
    core = li % NC
    z = (li // NC) % NZ
    x = li // (NC * NZ)

    def partner(k):
        dz, dc = k // NC, k % NC
        return (xor(x, xor(y, dz % 4, 2), 2) * NZ + xor(z, dz, 3)) * NC + (core + dc) % NC

    def peer(j):
        return (y + j) % NY

    barrier = pltpu.get_barrier_semaphore()
    for j in (1, 2, 3):
        pl.semaphore_signal(barrier, inc=1, device_id=(li, peer(j)), device_id_type=MESH)
    sibling = (li + 1 - 2 * core, y)
    pl.semaphore_signal(barrier, inc=1, device_id=sibling, device_id_type=MESH)

    @pl.when(y != 0)
    def _():
        pl.semaphore_signal(barrier, inc=1, device_id=(partner(0), y), device_id_type=MESH)

    def sig(k, c):
        pl.semaphore_signal(barrier, inc=1, device_id=(partner(k), y), device_id_type=MESH)
        return c

    lax.fori_loop(1, nk, sig, 0)

    slab_copies = [pltpu.make_async_copy(slab_hbm.at[l], slab.at[l], slab_sem.at[l]) for l in range(2)]
    for c in slab_copies:
        c.start()

    nl = 2 * nk
    row = lax.broadcasted_iota(jnp.int32, (nl, q_ref.shape[0]), 0)
    kk = row // 2
    dz = kk // NC
    xd = x ^ y ^ (dz & 3)
    zd = z ^ dz
    cd = (core + kk) % NC
    lvec = ((xd * NZ + zd) * NC + cd) * 2 + row % 2
    hit = probes_ref[0:1, :] == lvec
    for j in range(1, 4):
        hit = hit | (probes_ref[j : j + 1, :] == lvec)
    hits = jnp.where(hit, 1.0, 0.0).astype(F32)
    qn = q_ref.shape[0]
    before = jnp.where(
        lax.broadcasted_iota(jnp.int32, (qn, qn), 0) < lax.broadcasted_iota(jnp.int32, (qn, qn), 1), 1.0, 0.0
    ).astype(BF16)
    rank = jnp.dot(hits.astype(BF16), before, preferred_element_type=F32)
    rank = jnp.where(hit, rank, -1.0)
    slot = lax.broadcasted_iota(jnp.int32, (CAP, qn), 0).astype(F32)
    for r in range(nl):
        onehot[r // 2, r % 2] = jnp.where(rank[r : r + 1, :] == slot, 1.0, 0.0).astype(BF16)
    oh = onehot[...].reshape(nl * CAP, qn)
    picked = jnp.dot(oh, q_ref[...], preferred_element_type=F32) * (1.0 / math.sqrt(feat))
    send_q[...] = picked.astype(BF16).reshape(send_q.shape)
    own8 = jnp.broadcast_to((owner_ref[...] + 1).astype(F32), (8, qn)).astype(BF16)
    for i in range(2):
        send_o[i : i + 1, :] = nt_dot(own8, onehot[:, i].reshape(nq, qn))[0:1, :]
    bi[y] = jnp.broadcast_to(bias_ref[...].astype(F32), (8, bias_ref.shape[1]))

    onehot_t[...] = oh.astype(F32).T.astype(BF16)
    kt[:, :, feat : feat + 16, :] = jnp.ones((2, ntile, 16, tile), BF16)
    ptile = min(tile, 512)
    for l in range(2):
        slab_copies[l].wait()

        def prep(t, c):
            rows_t = slab[l, pl.ds(t * ptile, ptile), :]
            kt[l, t // (tile // ptile), 0:feat, pl.ds(t % (tile // ptile) * ptile, ptile)] = rows_t.astype(F32).T.astype(BF16)
            for h in range(ptile // 128):
                rr = rowner_ref[l : l + 1, pl.ds(t * ptile + h * 128, 128)].astype(F32)
                rcol[l, pl.ds(t * ptile + h * 128, 128), :] = jnp.broadcast_to(rr, (128, 128)).T
            return c

        lax.fori_loop(0, rows // ptile, prep, 0)

    pl.semaphore_wait(barrier, 4 + nk - (1 - (y + 3) // 4))

    def q_copy(k):
        return pltpu.make_async_remote_copy(
            src_ref=send_q.at[k], dst_ref=recv_q.at[y, k], send_sem=a2a_s.at[k], recv_sem=a2a_r.at[k],
            device_id=(partner(k), y), device_id_type=MESH)

    def o_copy(k):
        return pltpu.make_async_remote_copy(
            src_ref=send_o, dst_ref=recv_o.at[k], send_sem=o_s.at[k], recv_sem=o_r.at[k],
            device_id=(partner(k), y), device_id_type=MESH)

    q_self = pltpu.make_async_copy(send_q.at[0], recv_q.at[y, 0], a2a_r.at[0])
    o_self = pltpu.make_async_copy(send_o, recv_o.at[0], o_r.at[0])

    @pl.when(y == 0)
    def _():
        q_self.start()
        o_self.start()

    @pl.when(y != 0)
    def _():
        q_copy(0).start()
        o_copy(0).start()

    def a2a_start(k, c):
        q_copy(k).start()
        o_copy(k).start()
        return c

    lax.fori_loop(1, nk, a2a_start, 0)

    ih, oh2 = 2 * feat // NC, wo.shape[1] // NC
    in_half = pl.ds(pl.multiple_of(core * ih, ih), ih)
    out_half = pl.ds(pl.multiple_of(core * oh2, oh2), oh2)

    def w_copies(j):
        return [
            pltpu.make_async_remote_copy(
                src_ref=s, dst_ref=d, send_sem=w_s.at[n, j - 1], recv_sem=w_r.at[n, j - 1],
                device_id=(li, peer(j)), device_id_type=MESH)
            for n, (s, d) in enumerate((
                (win_ref.at[in_half], wi.at[y, in_half]),
                (wout_ref.at[out_half], wo.at[y, out_half]),
                (bi.at[y], bi.at[y])))
        ]

    def share_copies(j):
        src = peer(NY - j)
        return [
            pltpu.make_async_remote_copy(
                src_ref=d, dst_ref=d, send_sem=f_s.at[n, j - 1], recv_sem=f_r.at[n, j - 1],
                device_id=sibling, device_id_type=MESH)
            for n, d in enumerate((wi.at[src, in_half], wo.at[src, out_half]))
        ]

    weight_copies = [c for j in (1, 3, 2) for c in w_copies(j)]
    for c in weight_copies:
        c.start()
    local = [pltpu.make_async_copy(win_ref, wi.at[y], loc_sem.at[0]), pltpu.make_async_copy(wout_ref, wo.at[y], loc_sem.at[1])]
    for c in local:
        c.start()

    part_of = (pl.ds(0, nk // 2), pl.ds(nk // 2, nk // 2))

    def near_copy(j, p):
        return pltpu.make_async_remote_copy(
            src_ref=recv_q.at[y, part_of[p]], dst_ref=recv_q.at[y, part_of[p]],
            send_sem=ag_s.at[j - 1, p], recv_sem=ag_r.at[j - 1, p],
            device_id=(li, peer(j)), device_id_type=MESH)

    def far_copy(p):
        src, dst = (peer(3), peer(1)) if p == 0 else (peer(1), peer(3))
        return pltpu.make_async_remote_copy(
            src_ref=recv_q.at[src, part_of[p]], dst_ref=recv_q.at[src, part_of[p]],
            send_sem=ag_s.at[1, p], recv_sem=ag_r.at[1, p],
            device_id=(li, dst), device_id_type=MESH)

    def owners_copy(j):
        return pltpu.make_async_remote_copy(
            src_ref=own_o.at[y], dst_ref=own_o.at[y], send_sem=ago_s.at[j - 1], recv_sem=ago_r.at[j - 1],
            device_id=(li, peer(j)), device_id_type=MESH)

    @pl.when(y == 0)
    def _():
        q_self.wait()

    @pl.when(y != 0)
    def _():
        q_copy(0).wait()

    def a2a_wait(k, c):
        q_copy(k).wait()
        return c

    lax.fori_loop(1, nk // 2, a2a_wait, 0)
    for j in (1, 3):
        near_copy(j, 0).start()
    lax.fori_loop(nk // 2, nk, a2a_wait, 0)
    for j in (1, 3):
        near_copy(j, 1).start()

    @pl.when(y == 0)
    def _():
        o_self.wait()

    @pl.when(y != 0)
    def _():
        o_copy(0).wait()

    def o_wait(k, c):
        o_copy(k).wait()
        return c

    lax.fori_loop(1, nk, o_wait, 0)
    lane_k = lax.broadcasted_iota(jnp.int32, (2, nq), 1) // CAP
    total_o = jnp.zeros((2, nq), F32)
    for k in range(nk):
        total_o = total_o + jnp.where(lane_k == k, recv_o[k], 0.0)
    own_o[y] = total_o - 1.0
    for j in (1, 3, 2):
        owners_copy(j).start()

    order = [(0, 0), (0, 1), (1, 0), (3, 0), (2, 0), (1, 1), (3, 1), (2, 1)]
    arrived = {0}
    rs_sends = []

    def rs_copies(j, l):
        dev = (li, peer(j))
        return [
            pltpu.make_async_remote_copy(
                src_ref=part.at[peer(j), l], dst_ref=rpart.at[j - 1, l], send_sem=rs_s.at[j - 1, l],
                recv_sem=rs_r.at[j - 1, l], device_id=dev, device_id_type=MESH),
            pltpu.make_async_remote_copy(
                src_ref=lse.at[peer(j), l], dst_ref=rlse.at[j - 1, l], send_sem=rl_s.at[j - 1, l],
                recv_sem=rl_r.at[j - 1, l], device_id=dev, device_id_type=MESH),
        ]

    def score_tile(n, l, t, own_row, m):
        s = jnp.dot(slab[l, pl.ds(t * tile, tile), :], qt[n % 2], preferred_element_type=F32)
        rc = rcol[l, pl.ds(t * tile, tile), :]
        halves = []
        for h in range(nq // 128):
            cols = slice(h * 128, (h + 1) * 128)
            sh = s[:, cols]
            sh = jnp.where(rc == own_row[:, cols], sh - SCORE_PEN, sh)
            scores[n % 2, t, :, cols] = sh
            halves.append(jnp.max(sh.reshape(tile // 8, 8, 128), axis=0))
        return jnp.maximum(m, jnp.concatenate(halves, axis=1))

    def sum_tile(n, l, t, peak):
        w = jnp.exp2(((scores[n % 2, t] - peak) * LOG2E).astype(BF16))
        acc[...] += jnp.dot(kt[l, t], w, preferred_element_type=F32)

    peak = None
    for n in range(len(order) + 1):
        own_row = None
        if n < len(order):
            j, l = order[n]
            src = peer(NY - j)
            if j not in arrived:
                if j == 1:
                    near_copy(1, 0).wait_recv()
                    far_copy(0).start()
                    near_copy(3, 0).wait_recv()
                    near_copy(3, 1).wait_recv()
                    far_copy(1).start()
                    near_copy(1, 1).wait_recv()
                if j == 2:
                    far_copy(0).wait_recv()
                    far_copy(1).wait_recv()
                owners_copy(j).wait_recv()
                arrived.add(j)
            src = peer(NY - j)
            qt[n % 2] = recv_q[src, :, l].reshape(nq, feat).astype(F32).T.astype(BF16)
            own_row = own_o[src, l : l + 1, :]
        if n > 0:
            acc[...] = jnp.zeros_like(acc)
        prev_peak = peak

        def stage(t, m, n=n, own_row=own_row, prev_peak=prev_peak):
            if n > 0:
                sum_tile(n - 1, order[n - 1][1], t, prev_peak)
            if n < len(order):
                m = score_tile(n, order[n][1], t, own_row, m)
            return m

        if n == len(order) - 1:
            for c in weight_copies:
                c.wait()
            for j in (1, 2, 3):
                for c in share_copies(j):
                    c.start()
        m = lax.fori_loop(0, ntile, stage, jnp.full((8, nq), -jnp.inf, F32))
        if n > 0:
            pj, pl_ = order[n - 1]
            psrc = peer(NY - pj)
            total = acc[feat : feat + 1, :]
            mean = acc[0:feat, :] / total
            part[psrc, pl_] = mean.T.astype(BF16)
            lse[psrc, pl_] = prev_peak + jnp.log(total)
            if pj != 0:
                for c in rs_copies(NY - pj, pl_):
                    c.start()
                    rs_sends.append(c)
        if n < len(order):
            peak = jnp.max(m, axis=0, keepdims=True)

    def ret_copy(k, l):
        return pltpu.make_async_remote_copy(
            src_ref=ctx.at[k, l], dst_ref=ret.at[k, l], send_sem=ret_s.at[k, l], recv_sem=ret_r.at[k, l],
            device_id=(partner(k), y), device_id_type=MESH)

    def ret_self(l):
        return pltpu.make_async_copy(ctx.at[0, l], ret.at[0, l], ret_r.at[0, l])

    for l in range(2):
        for j in (1, 3, 2):
            for c in rs_copies(j, l):
                c.wait_recv()
        ls = [lse[y, l]] + [rlse[j - 1, l] for j in (1, 2, 3)]
        top = jnp.maximum(jnp.maximum(ls[0], ls[1]), jnp.maximum(ls[2], ls[3]))
        es = [jnp.exp(v - top) for v in ls]
        inv = 1.0 / (es[0] + es[1] + es[2] + es[3])
        cols = [jnp.broadcast_to(e * inv, (128, nq)).T for e in es]
        srcs = [part[y, l]] + [rpart[j - 1, l] for j in (1, 2, 3)]
        for h in range(feat // 128):
            cs = slice(h * 128, (h + 1) * 128)
            val = cols[0] * srcs[0][:, cs].astype(F32)
            for a in range(1, 4):
                val = val + cols[a] * srcs[a][:, cs].astype(F32)
            ctx[:, l, :, cs] = val.astype(BF16).reshape(nk, CAP, 128)

        @pl.when(y == 0)
        def _(l=l):
            ret_self(l).start()

        @pl.when(y != 0)
        def _(l=l):
            ret_copy(0, l).start()

        def ret_start(k, c, l=l):
            ret_copy(k, l).start()
            return c

        lax.fori_loop(1, nk, ret_start, 0)

    for l in range(2):

        @pl.when(y == 0)
        def _(l=l):
            ret_self(l).wait()

        @pl.when(y != 0)
        def _(l=l):
            ret_copy(0, l).wait()

        def ret_wait(k, c, l=l):
            ret_copy(k, l).wait()
            return c

        lax.fori_loop(1, nk, ret_wait, 0)

    share = jnp.dot(onehot_t[...], ret[...].reshape(nl * CAP, feat), preferred_element_type=F32) * 0.25
    qb = qn // NY
    pq[...] = share.astype(BF16).reshape(NY, qb, feat)
    pq_copies = {}
    for j in (1, 2, 3):
        pq_copies[j] = pltpu.make_async_remote_copy(
            src_ref=pq.at[peer(j)], dst_ref=rpq.at[j - 1], send_sem=pq_s.at[j - 1], recv_sem=pq_r.at[j - 1],
            device_id=(li, peer(j)), device_id_type=MESH)
        pq_copies[j].start()
    for j in (1, 2, 3):
        for c in share_copies(j):
            c.wait()
    for c in local:
        c.wait()
    mine = q_ref[pl.ds(pl.multiple_of(y * qb, qb), qb), :]
    for j in (1, 2, 3):
        pq_copies[j].wait()
    retrieved = pq[y].astype(F32)
    for j in (1, 2, 3):
        retrieved = retrieved + rpq[j - 1].astype(F32)
    normed = retrieved * lax.rsqrt(jnp.mean(retrieved * retrieved, axis=1, keepdims=True) + 1e-06)
    normed = normed.astype(BF16)
    res = jnp.zeros((qb, feat), F32)
    for b in range(NY):
        hid = jnp.dot(mine, wi[b, 0:feat, :], preferred_element_type=F32)
        hid = hid + jnp.dot(normed, wi[b, feat : 2 * feat, :], preferred_element_type=F32)
        hid = jax.nn.gelu(hid + bi[b, 0:1, :], approximate=True).astype(BF16)
        res = res + jnp.dot(hid, wo[b], preferred_element_type=F32)
    ob = feat // NY
    for b in range(NY):
        blk[b, :, 0:ob] = res[:, b * ob : (b + 1) * ob].astype(BF16)
        blk[b, :, ob:128] = jnp.zeros((qb, 128 - ob), BF16)
    blk_copies = {}
    for j in (1, 2, 3):
        blk_copies[j] = pltpu.make_async_remote_copy(
            src_ref=blk.at[peer(j)], dst_ref=rblk.at[y], send_sem=blk_s.at[j - 1], recv_sem=blk_r.at[j - 1],
            device_id=(li, peer(j)), device_id_type=MESH)
        blk_copies[j].start()
    out_ref[pl.ds(pl.multiple_of(y * qb, qb), qb), :] = blk[y][:, 0:ob]
    for p in range(2):
        for j in (1, 3):
            near_copy(j, p).wait_send()
        far_copy(p).wait_send()
    for j in (1, 2, 3):
        owners_copy(j).wait_send()
    for c in rs_sends:
        c.wait_send()
    for j in (1, 2, 3):
        blk_copies[j].wait()
        src = peer(NY - j)
        out_ref[pl.ds(pl.multiple_of(src * qb, qb), qb), :] = rblk[src][:, 0:ob]


def body(queries, query_owner, probes, list_slab, row_owner, proj_in, bias_in, proj_out):
    qn, feat = queries.shape
    lists, rows = list_slab.shape[0], list_slab.shape[1]
    nk = NZ * NC
    nq = nk * CAP
    nl = 2 * nk
    tile = min(TILE, rows)
    nt = rows // tile
    hid = proj_in.shape[1]
    qb = qn // NY
    vm = pltpu.VMEM
    dma = pltpu.SemaphoreType.DMA
    vspec = pl.BlockSpec(memory_space=pltpu.VMEM)
    return pl.pallas_call(
        kernel,
        out_shape=jax.ShapeDtypeStruct((qn, feat // NY), BF16),
        in_specs=[vspec, vspec, vspec, pl.BlockSpec(memory_space=pl.ANY), vspec, vspec, vspec, vspec],
        out_specs=vspec,
        scratch_shapes=[
            vm((lists, rows, feat), BF16),
            vm((lists, nt, feat + 16, tile), BF16),
            vm((lists, rows, 128), F32),
            vm((nk, 2, CAP, qn), BF16),
            vm((qn, nl * CAP), BF16),
            vm((nk, 2, CAP, feat), BF16),
            vm((2, nq), F32),
            vm((NY, nk, 2, CAP, feat), BF16),
            vm((nk, 2, nq), F32),
            vm((NY, 2, nq), F32),
            vm((2, feat, nq), BF16),
            vm((2, nt, tile, nq), F32),
            vm((feat + 16, nq), F32),
            vm((NY, 2, nq, feat), BF16),
            vm((NY, 2, 1, nq), F32),
            vm((NY - 1, 2, nq, feat), BF16),
            vm((NY - 1, 2, 1, nq), F32),
            vm((nk, 2, CAP, feat), BF16),
            vm((nk, 2, CAP, feat), BF16),
            vm((NY, qb, feat), BF16),
            vm((NY - 1, qb, feat), BF16),
            vm((NY, qb, 128), BF16),
            vm((NY, qb, 128), BF16),
            vm((NY, 2 * feat, hid), BF16),
            vm((NY, hid, feat), BF16),
            vm((NY, 8, hid), F32),
            dma((2,)),
            dma((nk,)), dma((nk,)), dma((nk,)), dma((nk,)),
            dma((3, 2)), dma((3, 2)), dma((3,)), dma((3,)),
            dma((3, 3)), dma((3, 3)),
            dma((3, 2)), dma((3, 2)), dma((3, 2)), dma((3, 2)),
            dma((2, 3)), dma((2, 3)), dma((nk, 2)), dma((nk, 2)),
            dma((3,)), dma((3,)), dma((3,)), dma((3,)),
            dma((2,)),
        ],
        compiler_params=pltpu.CompilerParams(
            collective_id=0, has_side_effects=True, vmem_limit_bytes=56 * 1024 * 1024
        ),
    )(queries, query_owner.reshape(1, qn), probes.T, list_slab, row_owner, proj_in, bias_in.reshape(1, hid), proj_out)


def solution(mesh):
    in_specs = (
        P("list", None),
        P("list"),
        P("list", None),
        P("list", "row", None),
        P("list", "row"),
        P(None, "row"),
        P("row"),
        P("row", None),
    )
    out_specs = P("list", "row")
    return jax.shard_map(body, mesh=mesh, in_specs=in_specs, out_specs=out_specs, check_vma=False)
```

```python
import math

import jax
import jax.numpy as jnp
from jax import lax
from jax.experimental import pallas as pl
from jax.experimental.pallas import tpu as pltpu
from jax.sharding import PartitionSpec as P

SCORE_PEN = 10000.0
LOG2E = math.log2(math.e)
NX, NZ, NC, NY = 4, 8, 2, 4
CAP = 16
TILE = 2048
MESH = pl.DeviceIdType.MESH
F32 = jnp.float32
BF16 = jnp.bfloat16


def xor(a, b, bits):
    out = 0
    for i in range(bits):
        out = out + ((a // 2**i + b // 2**i) % 2) * 2**i
    return out


def nt_dot(a, b):
    return lax.dot_general(a, b, (((1,), (1,)), ((), ())), preferred_element_type=F32)


def kernel(
    q_ref, owner_ref, probes_ref, slab_hbm, rowner_hbm, win_ref, bias_ref, wout_ref,
    out_ref,
    slab, rowner_ref, kt, rcol, onehot, onehot_t, send_q, send_o, recv_q, recv_o, own_o, qt, scores, acc,
    part, lse, rpart, rlse, ctx, ret, pq, rpq, blk, rblk, wi, wo, bi,
    slab_sem, a2a_s, a2a_r, o_s, o_r, ag_s, ag_r, ago_s, ago_r, w_s, w_r, rs_s, rs_r, rl_s, rl_r,
    f_s, f_r, ret_s, ret_r, pq_s, pq_r, blk_s, blk_r, loc_sem,
):
    nk = NZ * NC
    nq = nk * CAP
    rows = slab.shape[1]
    feat = slab.shape[2]
    tile = scores.shape[2]
    ntile = rows // tile
    li = lax.axis_index("list")
    y = lax.axis_index("row")
    core = li % NC
    z = (li // NC) % NZ
    x = li // (NC * NZ)

    def partner(k):
        dz, dc = k // NC, k % NC
        return (xor(x, xor(y, dz % 4, 2), 2) * NZ + xor(z, dz, 3)) * NC + (core + dc) % NC

    def peer(j):
        return (y + j) % NY

    barrier = pltpu.get_barrier_semaphore()
    for j in (1, 2, 3):
        pl.semaphore_signal(barrier, inc=1, device_id=(li, peer(j)), device_id_type=MESH)
    sibling = (li + 1 - 2 * core, y)
    pl.semaphore_signal(barrier, inc=1, device_id=sibling, device_id_type=MESH)

    @pl.when(y != 0)
    def _():
        pl.semaphore_signal(barrier, inc=1, device_id=(partner(0), y), device_id_type=MESH)

    def sig(k, c):
        pl.semaphore_signal(barrier, inc=1, device_id=(partner(k), y), device_id_type=MESH)
        return c

    lax.fori_loop(1, nk, sig, 0)

    slab_copies = [pltpu.make_async_copy(slab_hbm.at[l], slab.at[l], slab_sem.at[l]) for l in range(2)]
    slab_copies.append(pltpu.make_async_copy(rowner_hbm, rowner_ref, slab_sem.at[2]))
    for c in slab_copies:
        c.start()

    nl = 2 * nk
    row = lax.broadcasted_iota(jnp.int32, (nl, q_ref.shape[0]), 0)
    kk = row // 2
    dz = kk // NC
    xd = x ^ y ^ (dz & 3)
    zd = z ^ dz
    cd = (core + kk) % NC
    lvec = ((xd * NZ + zd) * NC + cd) * 2 + row % 2
    hit = probes_ref[0:1, :] == lvec
    for j in range(1, 4):
        hit = hit | (probes_ref[j : j + 1, :] == lvec)
    hits = jnp.where(hit, 1.0, 0.0).astype(F32)
    qn = q_ref.shape[0]
    before = jnp.where(
        lax.broadcasted_iota(jnp.int32, (qn, qn), 0) < lax.broadcasted_iota(jnp.int32, (qn, qn), 1), 1.0, 0.0
    ).astype(BF16)
    rank = jnp.dot(hits.astype(BF16), before, preferred_element_type=F32)
    rank = jnp.where(hit, rank, -1.0)
    slot = lax.broadcasted_iota(jnp.int32, (CAP, qn), 0).astype(F32)
    for r in range(nl):
        onehot[r // 2, r % 2] = jnp.where(rank[r : r + 1, :] == slot, 1.0, 0.0).astype(BF16)
    def pick(p):
        half = onehot[p * nk // 2 : (p + 1) * nk // 2].reshape(nq, qn)
        picked = jnp.dot(half, q_ref[...], preferred_element_type=F32) * (1.0 / math.sqrt(feat))
        send_q[p * nk // 2 : (p + 1) * nk // 2] = picked.astype(BF16).reshape(nk // 2, 2, CAP, feat)

    pick(0)
    pl.semaphore_wait(barrier, 4 + nk - (1 - (y + 3) // 4))

    def q_copy(k):
        return pltpu.make_async_remote_copy(
            src_ref=send_q.at[k], dst_ref=recv_q.at[y, k], send_sem=a2a_s.at[k], recv_sem=a2a_r.at[k],
            device_id=(partner(k), y), device_id_type=MESH)

    def o_copy(k):
        return pltpu.make_async_remote_copy(
            src_ref=send_o, dst_ref=recv_o.at[k], send_sem=o_s.at[k], recv_sem=o_r.at[k],
            device_id=(partner(k), y), device_id_type=MESH)

    q_self = pltpu.make_async_copy(send_q.at[0], recv_q.at[y, 0], a2a_r.at[0])
    o_self = pltpu.make_async_copy(send_o, recv_o.at[0], o_r.at[0])

    @pl.when(y == 0)
    def _():
        q_self.start()

    @pl.when(y != 0)
    def _():
        q_copy(0).start()

    def q_start(k, c):
        q_copy(k).start()
        return c

    def o_start(k, c):
        o_copy(k).start()
        return c

    lax.fori_loop(1, nk // 2, q_start, 0)
    pick(1)
    lax.fori_loop(nk // 2, nk, q_start, 0)
    own8 = jnp.broadcast_to((owner_ref[...] + 1).astype(F32), (8, qn)).astype(BF16)
    for i in range(2):
        send_o[i : i + 1, :] = nt_dot(own8, onehot[:, i].reshape(nq, qn))[0:1, :]
    bi[y] = jnp.broadcast_to(bias_ref[...].astype(F32).reshape(1, bias_ref.shape[0]), (8, bias_ref.shape[0]))


    @pl.when(y == 0)
    def _():
        o_self.start()

    @pl.when(y != 0)
    def _():
        o_copy(0).start()

    lax.fori_loop(1, nk, o_start, 0)

    ih, oh2 = 2 * feat // NC, wo.shape[1] // NC
    in_half = pl.ds(pl.multiple_of(core * ih, ih), ih)
    out_half = pl.ds(pl.multiple_of(core * oh2, oh2), oh2)

    def w_copies(j):
        return [
            pltpu.make_async_remote_copy(
                src_ref=s, dst_ref=d, send_sem=w_s.at[n, j - 1], recv_sem=w_r.at[n, j - 1],
                device_id=(li, peer(j)), device_id_type=MESH)
            for n, (s, d) in enumerate((
                (win_ref.at[in_half], wi.at[y, in_half]),
                (wout_ref.at[out_half], wo.at[y, out_half]),
                (bi.at[y], bi.at[y])))
        ]

    def share_copies(j):
        src = peer(NY - j)
        return [
            pltpu.make_async_remote_copy(
                src_ref=d, dst_ref=d, send_sem=f_s.at[n, j - 1], recv_sem=f_r.at[n, j - 1],
                device_id=sibling, device_id_type=MESH)
            for n, d in enumerate((wi.at[src, in_half], wo.at[src, out_half]))
        ]

    weight_copies = {j: w_copies(j) for j in (1, 3, 2)}
    for j in (1, 3, 2):
        for c in weight_copies[j][1:]:
            c.start()
    local = [pltpu.make_async_copy(win_ref, wi.at[y], loc_sem.at[0]), pltpu.make_async_copy(wout_ref, wo.at[y], loc_sem.at[1])]
    for c in local:
        c.start()

    onehot_t[...] = onehot[...].reshape(nl * CAP, qn).astype(F32).T.astype(BF16)
    kt[:, :, feat : feat + 16, :] = jnp.ones((2, ntile, 16, tile), BF16)
    ptile = min(tile, 512)
    slab_copies[2].wait()
    for l in range(2):
        slab_copies[l].wait()

        def prep(t, c):
            rows_t = slab[l, pl.ds(t * ptile, ptile), :]
            kt[l, t // (tile // ptile), 0:feat, pl.ds(t % (tile // ptile) * ptile, ptile)] = rows_t.astype(F32).T.astype(BF16)
            for h in range(ptile // 128):
                rr = rowner_ref[l : l + 1, pl.ds(t * ptile + h * 128, 128)].astype(F32)
                rcol[l, pl.ds(t * ptile + h * 128, 128), :] = jnp.broadcast_to(rr, (128, 128)).T
            return c

        lax.fori_loop(0, rows // ptile, prep, 0)

    part_of = (pl.ds(0, nk // 2), pl.ds(nk // 2, nk // 2))

    def near_copy(j, p):
        return pltpu.make_async_remote_copy(
            src_ref=recv_q.at[y, part_of[p]], dst_ref=recv_q.at[y, part_of[p]],
            send_sem=ag_s.at[j - 1, p], recv_sem=ag_r.at[j - 1, p],
            device_id=(li, peer(j)), device_id_type=MESH)

    def far_copy(p):
        src, dst = (peer(3), peer(1)) if p == 0 else (peer(1), peer(3))
        return pltpu.make_async_remote_copy(
            src_ref=recv_q.at[src, part_of[p]], dst_ref=recv_q.at[src, part_of[p]],
            send_sem=ag_s.at[1, p], recv_sem=ag_r.at[1, p],
            device_id=(li, dst), device_id_type=MESH)

    def owners_copy(j):
        return pltpu.make_async_remote_copy(
            src_ref=own_o.at[y], dst_ref=own_o.at[y], send_sem=ago_s.at[j - 1], recv_sem=ago_r.at[j - 1],
            device_id=(li, peer(j)), device_id_type=MESH)

    @pl.when(y == 0)
    def _():
        q_self.wait()

    @pl.when(y != 0)
    def _():
        q_copy(0).wait()

    def a2a_wait(k, c):
        q_copy(k).wait()
        return c

    lax.fori_loop(1, nk // 2, a2a_wait, 0)
    for j in (1, 3):
        near_copy(j, 0).start()
    lax.fori_loop(nk // 2, nk, a2a_wait, 0)
    for j in (1, 3):
        near_copy(j, 1).start()

    @pl.when(y == 0)
    def _():
        o_self.wait()

    @pl.when(y != 0)
    def _():
        o_copy(0).wait()

    def o_wait(k, c):
        o_copy(k).wait()
        return c

    lax.fori_loop(1, nk, o_wait, 0)
    lane_k = lax.broadcasted_iota(jnp.int32, (2, nq), 1) // CAP
    total_o = jnp.zeros((2, nq), F32)
    for k in range(nk):
        total_o = total_o + jnp.where(lane_k == k, recv_o[k], 0.0)
    own_o[y] = total_o - 1.0
    for j in (1, 3, 2):
        owners_copy(j).start()

    order = [(0, 0), (0, 1), (1, 0), (3, 0), (1, 1), (2, 0), (2, 1), (3, 1)]
    arrived = {0}
    rs_sends = []

    def rs_copies(j, l):
        dev = (li, peer(j))
        return [
            pltpu.make_async_remote_copy(
                src_ref=part.at[peer(j), l], dst_ref=rpart.at[j - 1, l], send_sem=rs_s.at[j - 1, l],
                recv_sem=rs_r.at[j - 1, l], device_id=dev, device_id_type=MESH),
            pltpu.make_async_remote_copy(
                src_ref=lse.at[peer(j), l], dst_ref=rlse.at[j - 1, l], send_sem=rl_s.at[j - 1, l],
                recv_sem=rl_r.at[j - 1, l], device_id=dev, device_id_type=MESH),
        ]

    def score_tile(n, l, t, own_row, m):
        s = jnp.dot(slab[l, pl.ds(t * tile, tile), :], qt[n % 2], preferred_element_type=F32)
        rc = rcol[l, pl.ds(t * tile, tile), :]
        halves = []
        for h in range(nq // 128):
            cols = slice(h * 128, (h + 1) * 128)
            sh = s[:, cols]
            sh = jnp.where(rc == own_row[:, cols], sh - SCORE_PEN, sh)
            scores[n % 2, t, :, cols] = sh
            halves.append(jnp.max(sh.reshape(tile // 8, 8, 128), axis=0))
        return jnp.maximum(m, jnp.concatenate(halves, axis=1))

    def sum_tile(n, l, t, peak):
        w = jnp.exp2(((scores[n % 2, t] - peak) * LOG2E).astype(BF16))
        acc[...] += jnp.dot(kt[l, t], w, preferred_element_type=F32)

    peak = None
    for n in range(len(order) + 1):
        own_row = None
        if n < len(order):
            j, l = order[n]
            src = peer(NY - j)
            if j not in arrived:
                if j == 1:
                    near_copy(1, 0).wait_recv()
                    far_copy(0).start()
                    near_copy(3, 0).wait_recv()
                    near_copy(3, 1).wait_recv()
                    far_copy(1).start()
                    near_copy(1, 1).wait_recv()
                if j == 2:
                    far_copy(0).wait_recv()
                    far_copy(1).wait_recv()
                owners_copy(j).wait_recv()
                arrived.add(j)
            src = peer(NY - j)
            qt[n % 2] = recv_q[src, :, l].reshape(nq, feat).astype(F32).T.astype(BF16)
            own_row = own_o[src, l : l + 1, :]
        if n > 0:
            acc[...] = jnp.zeros_like(acc)
        prev_peak = peak

        def stage(t, m, n=n, own_row=own_row, prev_peak=prev_peak):
            if n > 0:
                sum_tile(n - 1, order[n - 1][1], t, prev_peak)
            if n < len(order):
                m = score_tile(n, order[n][1], t, own_row, m)
            return m

        m = lax.fori_loop(0, ntile, stage, jnp.full((8, nq), -jnp.inf, F32))
        if n > 0:
            pj, pl_ = order[n - 1]
            psrc = peer(NY - pj)
            total = acc[feat : feat + 1, :]
            mean = acc[0:feat, :] / total
            part[psrc, pl_] = mean.T.astype(BF16)
            lse[psrc, pl_] = prev_peak + jnp.log(total)
            if pj != 0:
                for c in rs_copies(NY - pj, pl_):
                    c.start()
                    rs_sends.append(c)
        if n < len(order):
            peak = jnp.max(m, axis=0, keepdims=True)

    for j in (1, 3, 2):
        weight_copies[j][0].start()

    def ret_copy(k, l):
        return pltpu.make_async_remote_copy(
            src_ref=ctx.at[k, l], dst_ref=ret.at[k, l], send_sem=ret_s.at[k, l], recv_sem=ret_r.at[k, l],
            device_id=(partner(k), y), device_id_type=MESH)

    def ret_self(l):
        return pltpu.make_async_copy(ctx.at[0, l], ret.at[0, l], ret_r.at[0, l])

    for l in range(2):
        for j in (1, 3, 2):
            for c in rs_copies(j, l):
                c.wait_recv()
        ls = [lse[y, l]] + [rlse[j - 1, l] for j in (1, 2, 3)]
        top = jnp.maximum(jnp.maximum(ls[0], ls[1]), jnp.maximum(ls[2], ls[3]))
        es = [jnp.exp(v - top) for v in ls]
        inv = 1.0 / (es[0] + es[1] + es[2] + es[3])
        cols = [jnp.broadcast_to(e * inv, (128, nq)).T for e in es]
        srcs = [part[y, l]] + [rpart[j - 1, l] for j in (1, 2, 3)]
        for h in range(feat // 128):
            cs = slice(h * 128, (h + 1) * 128)
            val = cols[0] * srcs[0][:, cs].astype(F32)
            for a in range(1, 4):
                val = val + cols[a] * srcs[a][:, cs].astype(F32)
            ctx[:, l, :, cs] = val.astype(BF16).reshape(nk, CAP, 128)

        @pl.when(y == 0)
        def _(l=l):
            ret_self(l).start()

        @pl.when(y != 0)
        def _(l=l):
            ret_copy(0, l).start()

        def ret_start(k, c, l=l):
            ret_copy(k, l).start()
            return c

        lax.fori_loop(1, nk, ret_start, 0)

    for l in range(2):

        @pl.when(y == 0)
        def _(l=l):
            ret_self(l).wait()

        @pl.when(y != 0)
        def _(l=l):
            ret_copy(0, l).wait()

        def ret_wait(k, c, l=l):
            ret_copy(k, l).wait()
            return c

        lax.fori_loop(1, nk, ret_wait, 0)

    share = jnp.dot(onehot_t[...], ret[...].reshape(nl * CAP, feat), preferred_element_type=F32) * 0.25
    qb = qn // NY
    pq[...] = share.astype(BF16).reshape(NY, qb, feat)
    pq_copies = {}
    for j in (1, 2, 3):
        pq_copies[j] = pltpu.make_async_remote_copy(
            src_ref=pq.at[peer(j)], dst_ref=rpq.at[j - 1], send_sem=pq_s.at[j - 1], recv_sem=pq_r.at[j - 1],
            device_id=(li, peer(j)), device_id_type=MESH)
        pq_copies[j].start()
    for j in (1, 3, 2):
        for c in weight_copies[j]:
            c.wait()
        for c in share_copies(j):
            c.start()
    for j in (1, 3, 2):
        for c in share_copies(j):
            c.wait()
    for c in local:
        c.wait()
    mine = q_ref[pl.ds(pl.multiple_of(y * qb, qb), qb), :]
    for j in (1, 2, 3):
        pq_copies[j].wait()
    retrieved = pq[y].astype(F32)
    for j in (1, 2, 3):
        retrieved = retrieved + rpq[j - 1].astype(F32)
    normed = retrieved * lax.rsqrt(jnp.mean(retrieved * retrieved, axis=1, keepdims=True) + 1e-06)
    normed = normed.astype(BF16)
    res = jnp.zeros((qb, feat), F32)
    for b in range(NY):
        hid = jnp.dot(mine, wi[b, 0:feat, :], preferred_element_type=F32)
        hid = hid + jnp.dot(normed, wi[b, feat : 2 * feat, :], preferred_element_type=F32)
        hid = jax.nn.gelu(hid + bi[b, 0:1, :], approximate=True).astype(BF16)
        res = res + jnp.dot(hid, wo[b], preferred_element_type=F32)
    ob = feat // NY
    for b in range(NY):
        blk[b, :, 0:ob] = res[:, b * ob : (b + 1) * ob].astype(BF16)
        blk[b, :, ob:128] = jnp.zeros((qb, 128 - ob), BF16)
    blk_copies = {}
    for j in (1, 2, 3):
        blk_copies[j] = pltpu.make_async_remote_copy(
            src_ref=blk.at[peer(j)], dst_ref=rblk.at[y], send_sem=blk_s.at[j - 1], recv_sem=blk_r.at[j - 1],
            device_id=(li, peer(j)), device_id_type=MESH)
        blk_copies[j].start()
    rblk[y] = blk[y]
    for p in range(2):
        for j in (1, 3):
            near_copy(j, p).wait_send()
        far_copy(p).wait_send()
    for j in (1, 2, 3):
        owners_copy(j).wait_send()
    for c in rs_sends:
        c.wait_send()
    for j in (1, 2, 3):
        blk_copies[j].wait()
    full = rblk[...].reshape(qn, 128).astype(F32)
    out_ref[...] = full.T[0:ob, :].astype(BF16)


def body(queries, query_owner, probes, list_slab, row_owner, proj_in, bias_in, proj_out):
    qn, feat = queries.shape
    lists, rows = list_slab.shape[0], list_slab.shape[1]
    nk = NZ * NC
    nq = nk * CAP
    nl = 2 * nk
    tile = min(TILE, rows)
    nt = rows // tile
    hid = proj_in.shape[1]
    qb = qn // NY
    vm = pltpu.VMEM
    dma = pltpu.SemaphoreType.DMA
    vspec = pl.BlockSpec(memory_space=pltpu.VMEM)
    hbm = pl.BlockSpec(memory_space=pl.ANY)
    out_t = pl.pallas_call(
        kernel,
        out_shape=jax.ShapeDtypeStruct((feat // NY, qn), BF16),
        in_specs=[vspec, vspec, vspec, hbm, hbm, hbm, vspec, hbm],
        out_specs=vspec,
        scratch_shapes=[
            vm((lists, rows, feat), BF16),
            vm((lists, rows), jnp.int32),
            vm((lists, nt, feat + 16, tile), BF16),
            vm((lists, rows, 128), F32),
            vm((nk, 2, CAP, qn), BF16),
            vm((qn, nl * CAP), BF16),
            vm((nk, 2, CAP, feat), BF16),
            vm((2, nq), F32),
            vm((NY, nk, 2, CAP, feat), BF16),
            vm((nk, 2, nq), F32),
            vm((NY, 2, nq), F32),
            vm((2, feat, nq), BF16),
            vm((2, nt, tile, nq), F32),
            vm((feat + 16, nq), F32),
            vm((NY, 2, nq, feat), BF16),
            vm((NY, 2, 1, nq), F32),
            vm((NY - 1, 2, nq, feat), BF16),
            vm((NY - 1, 2, 1, nq), F32),
            vm((nk, 2, CAP, feat), BF16),
            vm((nk, 2, CAP, feat), BF16),
            vm((NY, qb, feat), BF16),
            vm((NY - 1, qb, feat), BF16),
            vm((NY, qb, 128), BF16),
            vm((NY, qb, 128), BF16),
            vm((NY, 2 * feat, hid), BF16),
            vm((NY, hid, feat), BF16),
            vm((NY, 8, hid), F32),
            dma((3,)),
            dma((nk,)), dma((nk,)), dma((nk,)), dma((nk,)),
            dma((3, 2)), dma((3, 2)), dma((3,)), dma((3,)),
            dma((3, 3)), dma((3, 3)),
            dma((3, 2)), dma((3, 2)), dma((3, 2)), dma((3, 2)),
            dma((2, 3)), dma((2, 3)), dma((nk, 2)), dma((nk, 2)),
            dma((3,)), dma((3,)), dma((3,)), dma((3,)),
            dma((2,)),
        ],
        compiler_params=pltpu.CompilerParams(
            collective_id=0, has_side_effects=True, vmem_limit_bytes=56 * 1024 * 1024
        ),
    )(queries, query_owner.reshape(1, qn), probes.T, list_slab, row_owner, proj_in, bias_in, proj_out)
    return out_t.T


def solution(mesh):
    in_specs = (
        P("list", None),
        P("list"),
        P("list", None),
        P("list", "row", None),
        P("list", "row"),
        P(None, "row"),
        P("row"),
        P("row", None),
    )
    out_specs = P("list", "row")
    return jax.shard_map(body, mesh=mesh, in_specs=in_specs, out_specs=out_specs, check_vma=False)
```

```python
import math

import jax
import jax.numpy as jnp
from jax import lax
from jax.experimental import pallas as pl
from jax.experimental.pallas import tpu as pltpu
from jax.sharding import PartitionSpec as P

SCORE_PEN = 10000.0
LOG2E = math.log2(math.e)
NX, NZ, NC, NY = 4, 8, 2, 4
CAP = 16
TILE = 2048
MESH = pl.DeviceIdType.MESH
F32 = jnp.float32
BF16 = jnp.bfloat16


def xor(a, b, bits):
    out = 0
    for i in range(bits):
        out = out + ((a // 2**i + b // 2**i) % 2) * 2**i
    return out


def nt_dot(a, b):
    return lax.dot_general(a, b, (((1,), (1,)), ((), ())), preferred_element_type=F32)


def kernel(
    q_ref, owner_ref, probes_ref, slab_hbm, rowner_hbm, win_ref, bias_ref, wout_ref,
    out_ref,
    slab, rowner_ref, kt, rcol, onehot, onehot_t, send_q, send_o, recv_q, recv_o, own_o, qt, scores, acc,
    part, lse, rpart, rlse, ctx, ret, pq, rpq, blk, rblk, wi, wo, bi,
    slab_sem, a2a_s, a2a_r, o_s, o_r, ag_s, ag_r, ago_s, ago_r, w_s, w_r, rs_s, rs_r, rl_s, rl_r,
    f_s, f_r, ret_s, ret_r, pq_s, pq_r, blk_s, blk_r, loc_sem,
):
    nk = NZ * NC
    nq = nk * CAP
    rows = slab.shape[1]
    feat = slab.shape[2]
    tile = scores.shape[2]
    ntile = rows // tile
    li = lax.axis_index("list")
    y = lax.axis_index("row")
    core = li % NC
    z = (li // NC) % NZ
    x = li // (NC * NZ)

    def partner(k):
        dz, dc = k // NC, k % NC
        return (xor(x, xor(y, dz % 4, 2), 2) * NZ + xor(z, dz, 3)) * NC + (core + dc) % NC

    def peer(j):
        return (y + j) % NY

    barrier = pltpu.get_barrier_semaphore()
    for j in (1, 2, 3):
        pl.semaphore_signal(barrier, inc=1, device_id=(li, peer(j)), device_id_type=MESH)
    sibling = (li + 1 - 2 * core, y)
    pl.semaphore_signal(barrier, inc=1, device_id=sibling, device_id_type=MESH)

    @pl.when(y != 0)
    def _():
        pl.semaphore_signal(barrier, inc=1, device_id=(partner(0), y), device_id_type=MESH)

    def sig(k, c):
        pl.semaphore_signal(barrier, inc=1, device_id=(partner(k), y), device_id_type=MESH)
        return c

    lax.fori_loop(1, nk, sig, 0)

    slab_copies = [pltpu.make_async_copy(slab_hbm.at[l], slab.at[l], slab_sem.at[l]) for l in range(2)]
    slab_copies.append(pltpu.make_async_copy(rowner_hbm, rowner_ref, slab_sem.at[2]))
    for c in slab_copies:
        c.start()

    nl = 2 * nk
    row = lax.broadcasted_iota(jnp.int32, (nl, q_ref.shape[0]), 0)
    kk = row % nk
    dz = kk // NC
    xd = x ^ y ^ (dz & 3)
    zd = z ^ dz
    cd = (core + kk) % NC
    lvec = ((xd * NZ + zd) * NC + cd) * 2 + row // nk
    hit = probes_ref[0:1, :] == lvec
    for j in range(1, 4):
        hit = hit | (probes_ref[j : j + 1, :] == lvec)
    hits = jnp.where(hit, 1.0, 0.0).astype(F32)
    qn = q_ref.shape[0]
    before = jnp.where(
        lax.broadcasted_iota(jnp.int32, (qn, qn), 0) < lax.broadcasted_iota(jnp.int32, (qn, qn), 1), 1.0, 0.0
    ).astype(BF16)
    rank = jnp.dot(hits.astype(BF16), before, preferred_element_type=F32)
    rank = jnp.where(hit, rank, -1.0)
    slot = lax.broadcasted_iota(jnp.int32, (CAP, qn), 0).astype(F32)
    for r in range(nl):
        onehot[r // nk, r % nk] = jnp.where(rank[r : r + 1, :] == slot, 1.0, 0.0).astype(BF16)
    def pick(l):
        picked = jnp.dot(onehot[l].reshape(nq, qn), q_ref[...], preferred_element_type=F32) * (1.0 / math.sqrt(feat))
        send_q[l] = picked.astype(BF16).reshape(nk, CAP, feat)

    pick(0)
    own8 = jnp.broadcast_to((owner_ref[...] + 1).astype(F32), (8, qn)).astype(BF16)
    for i in range(2):
        send_o[i : i + 1, :] = nt_dot(own8, onehot[i].reshape(nq, qn))[0:1, :]

    pl.semaphore_wait(barrier, 4 + nk - (1 - (y + 3) // 4))

    def q_copy(k, l):
        return pltpu.make_async_remote_copy(
            src_ref=send_q.at[l, k], dst_ref=recv_q.at[y, l, k], send_sem=a2a_s.at[l, k], recv_sem=a2a_r.at[l, k],
            device_id=(partner(k), y), device_id_type=MESH)

    def o_copy(k):
        return pltpu.make_async_remote_copy(
            src_ref=send_o, dst_ref=recv_o.at[k], send_sem=o_s.at[k], recv_sem=o_r.at[k],
            device_id=(partner(k), y), device_id_type=MESH)

    q_self = [pltpu.make_async_copy(send_q.at[l, 0], recv_q.at[y, l, 0], a2a_r.at[l, 0]) for l in range(2)]
    o_self = pltpu.make_async_copy(send_o, recv_o.at[0], o_r.at[0])

    def all_partners(alone, copy):
        @pl.when(y == 0)
        def _():
            alone()

        @pl.when(y != 0)
        def _():
            copy(0)

        def step(k, c):
            copy(k)
            return c

        lax.fori_loop(1, nk, step, 0)

    all_partners(q_self[0].start, lambda k: q_copy(k, 0).start())
    all_partners(o_self.start, lambda k: o_copy(k).start())
    pick(1)
    all_partners(q_self[1].start, lambda k: q_copy(k, 1).start())
    bi[y] = jnp.broadcast_to(bias_ref[...].astype(F32).reshape(1, bias_ref.shape[0]), (8, bias_ref.shape[0]))

    ih, oh2 = 2 * feat // NC, wo.shape[1] // NC
    in_half = pl.ds(pl.multiple_of(core * ih, ih), ih)
    out_half = pl.ds(pl.multiple_of(core * oh2, oh2), oh2)

    def w_copies(j):
        return [
            pltpu.make_async_remote_copy(
                src_ref=s, dst_ref=d, send_sem=w_s.at[n, j - 1], recv_sem=w_r.at[n, j - 1],
                device_id=(li, peer(j)), device_id_type=MESH)
            for n, (s, d) in enumerate((
                (win_ref.at[in_half], wi.at[y, in_half]),
                (wout_ref.at[out_half], wo.at[y, out_half]),
                (bi.at[y], bi.at[y])))
        ]

    def share_copies(j):
        src = peer(NY - j)
        return [
            pltpu.make_async_remote_copy(
                src_ref=d, dst_ref=d, send_sem=f_s.at[n, j - 1], recv_sem=f_r.at[n, j - 1],
                device_id=sibling, device_id_type=MESH)
            for n, d in enumerate((wi.at[src, in_half], wo.at[src, out_half]))
        ]

    weight_copies = {j: w_copies(j) for j in (1, 3, 2)}
    for j in (1, 3, 2):
        for c in weight_copies[j][1:]:
            c.start()
    local = [pltpu.make_async_copy(win_ref, wi.at[y], loc_sem.at[0]), pltpu.make_async_copy(wout_ref, wo.at[y], loc_sem.at[1])]
    for c in local:
        c.start()

    onehot_t[...] = onehot[...].reshape(nl * CAP, qn).astype(F32).T.astype(BF16)
    kt[:, :, feat : feat + 16, :] = jnp.ones((2, ntile, 16, tile), BF16)
    ptile = min(tile, 512)
    slab_copies[2].wait()
    for l in range(2):
        slab_copies[l].wait()

        def prep(t, c):
            rows_t = slab[l, pl.ds(t * ptile, ptile), :]
            kt[l, t // (tile // ptile), 0:feat, pl.ds(t % (tile // ptile) * ptile, ptile)] = rows_t.astype(F32).T.astype(BF16)
            for h in range(ptile // 128):
                rr = rowner_ref[l : l + 1, pl.ds(t * ptile + h * 128, 128)].astype(F32)
                rcol[l, pl.ds(t * ptile + h * 128, 128), :] = jnp.broadcast_to(rr, (128, 128)).T
            return c

        lax.fori_loop(0, rows // ptile, prep, 0)

    half_of = (pl.ds(0, nk // 2), pl.ds(nk // 2, nk // 2))

    def near_copy(j, l):
        return pltpu.make_async_remote_copy(
            src_ref=recv_q.at[y, l], dst_ref=recv_q.at[y, l],
            send_sem=ag_s.at[j - 1, l, 0], recv_sem=ag_r.at[j - 1, l, 0],
            device_id=(li, peer(j)), device_id_type=MESH)

    def far_copy(p, l):
        src, dst = (peer(3), peer(1)) if p == 0 else (peer(1), peer(3))
        return pltpu.make_async_remote_copy(
            src_ref=recv_q.at[src, l, half_of[p]], dst_ref=recv_q.at[src, l, half_of[p]],
            send_sem=ag_s.at[1, l, p], recv_sem=ag_r.at[1, l, p],
            device_id=(li, dst), device_id_type=MESH)

    def owners_copy(j):
        return pltpu.make_async_remote_copy(
            src_ref=own_o.at[y], dst_ref=own_o.at[y], send_sem=ago_s.at[j - 1], recv_sem=ago_r.at[j - 1],
            device_id=(li, peer(j)), device_id_type=MESH)

    def gather(j, l):
        if j == 0:
            all_partners(q_self[l].wait, lambda k: q_copy(k, l).wait())
            for d in (1, 3):
                near_copy(d, l).start()
            if l == 0:
                all_partners(o_self.wait, lambda k: o_copy(k).wait())
                lane_k = lax.broadcasted_iota(jnp.int32, (2, nq), 1) // CAP
                total_o = jnp.zeros((2, nq), F32)
                for k in range(nk):
                    total_o = total_o + jnp.where(lane_k == k, recv_o[k], 0.0)
                own_o[y] = total_o - 1.0
                for d in (1, 3, 2):
                    owners_copy(d).start()
        elif j == 1:
            near_copy(1, l).wait_recv()
            far_copy(0, l).start()
            near_copy(3, l).wait_recv()
            far_copy(1, l).start()
        elif j == 2:
            far_copy(0, l).wait_recv()
            far_copy(1, l).wait_recv()
        if j != 0 and l == 0:
            owners_copy(j).wait_recv()

    order = [(0, 0), (0, 1), (1, 0), (3, 0), (1, 1), (2, 0), (3, 1), (2, 1)]
    rs_sends = []

    rows_of = (pl.ds(0, nq // 2), pl.ds(nq // 2, nq // 2))

    def rs_copy(j, l, p):
        return pltpu.make_async_remote_copy(
            src_ref=part.at[peer(j), l, rows_of[p]], dst_ref=rpart.at[j - 1, l, rows_of[p]],
            send_sem=rs_s.at[j - 1, l, p], recv_sem=rs_r.at[j - 1, l, p],
            device_id=(li, peer(j)), device_id_type=MESH)

    def rl_copy(j, l):
        return pltpu.make_async_remote_copy(
            src_ref=lse.at[peer(j), l], dst_ref=rlse.at[j - 1, l], send_sem=rl_s.at[j - 1, l],
            recv_sem=rl_r.at[j - 1, l], device_id=(li, peer(j)), device_id_type=MESH)

    def score_tile(n, l, t, own_row, m):
        s = jnp.dot(slab[l, pl.ds(t * tile, tile), :], qt[n % 2], preferred_element_type=F32)
        rc = rcol[l, pl.ds(t * tile, tile), :]
        halves = []
        for h in range(nq // 128):
            cols = slice(h * 128, (h + 1) * 128)
            sh = s[:, cols]
            sh = jnp.where(rc == own_row[:, cols], sh - SCORE_PEN, sh)
            scores[n % 2, t, :, cols] = sh
            halves.append(jnp.max(sh.reshape(tile // 8, 8, 128), axis=0))
        return jnp.maximum(m, jnp.concatenate(halves, axis=1))

    def sum_tile(n, l, t, peak):
        w = jnp.exp2(((scores[n % 2, t] - peak) * LOG2E).astype(BF16))
        acc[...] += jnp.dot(kt[l, t], w, preferred_element_type=F32)

    peak = None
    for n in range(len(order) + 1):
        own_row = None
        if n < len(order):
            j, l = order[n]
            src = peer(NY - j)
            gather(j, l)
            src = peer(NY - j)
            qt[n % 2] = recv_q[src, l].reshape(nq, feat).astype(F32).T.astype(BF16)
            own_row = own_o[src, l : l + 1, :]
        if n > 0:
            acc[...] = jnp.zeros_like(acc)
        prev_peak = peak

        def stage(t, m, n=n, own_row=own_row, prev_peak=prev_peak):
            if n > 0:
                sum_tile(n - 1, order[n - 1][1], t, prev_peak)
            if n < len(order):
                m = score_tile(n, order[n][1], t, own_row, m)
            return m

        m = lax.fori_loop(0, ntile, stage, jnp.full((8, nq), -jnp.inf, F32))
        if n > 0:
            pj, pl_ = order[n - 1]
            psrc = peer(NY - pj)
            total = acc[feat : feat + 1, :]
            mean = acc[0:feat, :] / total
            part[psrc, pl_] = mean.T.astype(BF16)
            lse[psrc, pl_] = prev_peak + jnp.log(total)
            if pj != 0:
                for c in (rl_copy(NY - pj, pl_), rs_copy(NY - pj, pl_, 0), rs_copy(NY - pj, pl_, 1)):
                    c.start()
                    rs_sends.append(c)
        if n < len(order):
            peak = jnp.max(m, axis=0, keepdims=True)

    for j in (1, 3, 2):
        weight_copies[j][0].start()

    def ret_copy(k, l):
        return pltpu.make_async_remote_copy(
            src_ref=ctx.at[l, k], dst_ref=ret.at[l, k], send_sem=ret_s.at[l, k], recv_sem=ret_r.at[l, k],
            device_id=(partner(k), y), device_id_type=MESH)

    def ret_self(l):
        return pltpu.make_async_copy(ctx.at[l, 0], ret.at[l, 0], ret_r.at[l, 0])

    def part_partners(p, alone, copy):
        if p == 0:

            @pl.when(y == 0)
            def _():
                alone()

            @pl.when(y != 0)
            def _():
                copy(0)

        def step(k, c):
            copy(k)
            return c

        lax.fori_loop(max(1, p * nk // 2), (p + 1) * nk // 2, step, 0)

    for l in range(2):
        for j in (1, 3, 2):
            rl_copy(j, l).wait_recv()
        ls = [lse[y, l]] + [rlse[j - 1, l] for j in (1, 2, 3)]
        top = jnp.maximum(jnp.maximum(ls[0], ls[1]), jnp.maximum(ls[2], ls[3]))
        es = [jnp.exp(v - top) for v in ls]
        inv = 1.0 / (es[0] + es[1] + es[2] + es[3])
        cols = [jnp.broadcast_to(e * inv, (128, nq)).T for e in es]
        for p in range(2):
            for j in (1, 3, 2):
                rs_copy(j, l, p).wait_recv()
            rs = slice(p * nq // 2, (p + 1) * nq // 2)
            srcs = [part[y, l, rs]] + [rpart[j - 1, l, rs] for j in (1, 2, 3)]
            for h in range(feat // 128):
                cs = slice(h * 128, (h + 1) * 128)
                val = cols[0][rs] * srcs[0][:, cs].astype(F32)
                for a in range(1, 4):
                    val = val + cols[a][rs] * srcs[a][:, cs].astype(F32)
                ctx[l, p * nk // 2 : (p + 1) * nk // 2, :, cs] = val.astype(BF16).reshape(nk // 2, CAP, 128)
            part_partners(p, ret_self(l).start, lambda k, l=l: ret_copy(k, l).start())

    share = None
    for l in range(2):
        all_partners(ret_self(l).wait, lambda k, l=l: ret_copy(k, l).wait_recv())
        piece = jnp.dot(
            onehot_t[:, l * nq : (l + 1) * nq], ret[l].reshape(nq, feat), preferred_element_type=F32)
        share = piece if share is None else share + piece

    share = share * 0.25
    qb = qn // NY
    pq[...] = share.astype(BF16).reshape(NY, qb, feat)
    pq_copies = {}
    for j in (1, 2, 3):
        pq_copies[j] = pltpu.make_async_remote_copy(
            src_ref=pq.at[peer(j)], dst_ref=rpq.at[j - 1], send_sem=pq_s.at[j - 1], recv_sem=pq_r.at[j - 1],
            device_id=(li, peer(j)), device_id_type=MESH)
        pq_copies[j].start()
    for j in (1, 3, 2):
        for c in weight_copies[j]:
            c.wait()
        for c in share_copies(j):
            c.start()
    for j in (1, 3, 2):
        for c in share_copies(j):
            c.wait()
    for c in local:
        c.wait()
    mine = q_ref[pl.ds(pl.multiple_of(y * qb, qb), qb), :]
    hids = [jnp.dot(mine, wi[b, 0:feat, :], preferred_element_type=F32) + bi[b, 0:1, :] for b in range(NY)]
    for j in (1, 2, 3):
        pq_copies[j].wait()
    retrieved = pq[y].astype(F32)
    for j in (1, 2, 3):
        retrieved = retrieved + rpq[j - 1].astype(F32)
    normed = retrieved * lax.rsqrt(jnp.mean(retrieved * retrieved, axis=1, keepdims=True) + 1e-06)
    normed = normed.astype(BF16)
    res = jnp.zeros((qb, feat), F32)
    for b in range(NY):
        hid = hids[b] + jnp.dot(normed, wi[b, feat : 2 * feat, :], preferred_element_type=F32)
        hid = jax.nn.gelu(hid, approximate=True).astype(BF16)
        res = res + jnp.dot(hid, wo[b], preferred_element_type=F32)
    ob = feat // NY
    for b in range(NY):
        blk[b, :, 0:ob] = res[:, b * ob : (b + 1) * ob].astype(BF16)
        blk[b, :, ob:128] = jnp.zeros((qb, 128 - ob), BF16)
    blk_copies = {}
    for j in (1, 2, 3):
        blk_copies[j] = pltpu.make_async_remote_copy(
            src_ref=blk.at[peer(j)], dst_ref=rblk.at[y], send_sem=blk_s.at[j - 1], recv_sem=blk_r.at[j - 1],
            device_id=(li, peer(j)), device_id_type=MESH)
        blk_copies[j].start()
    rblk[y] = blk[y]
    for l in range(2):
        for j in (1, 3):
            near_copy(j, l).wait_send()
        for p in range(2):
            far_copy(p, l).wait_send()
    for j in (1, 2, 3):
        owners_copy(j).wait_send()
    for c in rs_sends:
        c.wait_send()
    for l in range(2):
        part_partners(1, None, lambda k, l=l: ret_copy(k, l).wait_send())

        @pl.when(y != 0)
        def _(l=l):
            ret_copy(0, l).wait_send()

        def ret_sent(k, c, l=l):
            ret_copy(k, l).wait_send()
            return c

        lax.fori_loop(1, nk // 2, ret_sent, 0)
    for j in (1, 2, 3):
        blk_copies[j].wait()
    full = rblk[...].reshape(qn, 128).astype(F32)
    out_ref[...] = full.T[0:ob, :].astype(BF16)


def body(queries, query_owner, probes, list_slab, row_owner, proj_in, bias_in, proj_out):
    qn, feat = queries.shape
    lists, rows = list_slab.shape[0], list_slab.shape[1]
    nk = NZ * NC
    nq = nk * CAP
    nl = 2 * nk
    tile = min(TILE, rows)
    nt = rows // tile
    hid = proj_in.shape[1]
    qb = qn // NY
    vm = pltpu.VMEM
    dma = pltpu.SemaphoreType.DMA
    vspec = pl.BlockSpec(memory_space=pltpu.VMEM)
    hbm = pl.BlockSpec(memory_space=pl.ANY)
    out_t = pl.pallas_call(
        kernel,
        out_shape=jax.ShapeDtypeStruct((feat // NY, qn), BF16),
        in_specs=[vspec, vspec, vspec, hbm, hbm, hbm, vspec, hbm],
        out_specs=vspec,
        scratch_shapes=[
            vm((lists, rows, feat), BF16),
            vm((lists, rows), jnp.int32),
            vm((lists, nt, feat + 16, tile), BF16),
            vm((lists, rows, 128), F32),
            vm((2, nk, CAP, qn), BF16),
            vm((qn, nl * CAP), BF16),
            vm((2, nk, CAP, feat), BF16),
            vm((2, nq), F32),
            vm((NY, 2, nk, CAP, feat), BF16),
            vm((nk, 2, nq), F32),
            vm((NY, 2, nq), F32),
            vm((2, feat, nq), BF16),
            vm((2, nt, tile, nq), F32),
            vm((feat + 16, nq), F32),
            vm((NY, 2, nq, feat), BF16),
            vm((NY, 2, 1, nq), F32),
            vm((NY - 1, 2, nq, feat), BF16),
            vm((NY - 1, 2, 1, nq), F32),
            vm((2, nk, CAP, feat), BF16),
            vm((2, nk, CAP, feat), BF16),
            vm((NY, qb, feat), BF16),
            vm((NY - 1, qb, feat), BF16),
            vm((NY, qb, 128), BF16),
            vm((NY, qb, 128), BF16),
            vm((NY, 2 * feat, hid), BF16),
            vm((NY, hid, feat), BF16),
            vm((NY, 8, hid), F32),
            dma((3,)),
            dma((2, nk)), dma((2, nk)), dma((nk,)), dma((nk,)),
            dma((3, 2, 2)), dma((3, 2, 2)), dma((3,)), dma((3,)),
            dma((3, 3)), dma((3, 3)),
            dma((3, 2, 2)), dma((3, 2, 2)), dma((3, 2)), dma((3, 2)),
            dma((2, 3)), dma((2, 3)), dma((2, nk)), dma((2, nk)),
            dma((3,)), dma((3,)), dma((3,)), dma((3,)),
            dma((2,)),
        ],
        compiler_params=pltpu.CompilerParams(
            collective_id=0, has_side_effects=True, vmem_limit_bytes=56 * 1024 * 1024
        ),
    )(queries, query_owner.reshape(1, qn), probes.T, list_slab, row_owner, proj_in, bias_in, proj_out)
    return out_t.T


def solution(mesh):
    in_specs = (
        P("list", None),
        P("list"),
        P("list", None),
        P("list", "row", None),
        P("list", "row"),
        P(None, "row"),
        P("row"),
        P("row", None),
    )
    out_specs = P("list", "row")
    return jax.shard_map(body, mesh=mesh, in_specs=in_specs, out_specs=out_specs, check_vma=False)
```

```python
import math

import jax
import jax.numpy as jnp
from jax import lax
from jax.experimental import pallas as pl
from jax.experimental.pallas import tpu as pltpu
from jax.sharding import PartitionSpec as P

SCORE_PEN = 10000.0
LOG2E = math.log2(math.e)
NX, NZ, NC, NY = 4, 8, 2, 4
CAP = 16
TILE = 2048
MESH = pl.DeviceIdType.MESH
F32 = jnp.float32
BF16 = jnp.bfloat16


def xor(a, b, bits):
    out = 0
    for i in range(bits):
        out = out + ((a // 2**i + b // 2**i) % 2) * 2**i
    return out


def nt_dot(a, b):
    return lax.dot_general(a, b, (((1,), (1,)), ((), ())), preferred_element_type=F32)


def kernel(
    q_ref, owner_ref, probes_ref, slab_hbm, rowner_hbm, win_ref, bias_ref, wout_ref,
    out_ref,
    slab, rowner_ref, kt, rcol, onehot, onehot_t, send_q, send_o, recv_q, recv_o, own_o, qt, scores, acc,
    part, lse, rpart, rlse, ctx, ret, pq, rpq, blk, rblk, wi, wo, bi,
    slab_sem, a2a_s, a2a_r, o_s, o_r, ag_s, ag_r, ago_s, ago_r, w_s, w_r, rs_s, rs_r, rl_s, rl_r,
    f_s, f_r, ret_s, ret_r, pq_s, pq_r, blk_s, blk_r, loc_sem,
):
    nk = NZ * NC
    nq = nk * CAP
    rows = slab.shape[1]
    feat = slab.shape[2]
    tile = scores.shape[2]
    ntile = rows // tile
    li = lax.axis_index("list")
    y = lax.axis_index("row")
    core = li % NC
    z = (li // NC) % NZ
    x = li // (NC * NZ)

    def partner(k):
        dz, dc = k // NC, k % NC
        return (xor(x, xor(y, dz % 4, 2), 2) * NZ + xor(z, dz, 3)) * NC + (core + dc) % NC

    def peer(j):
        return (y + j) % NY

    barrier = pltpu.get_barrier_semaphore()
    for j in (1, 2, 3):
        pl.semaphore_signal(barrier, inc=1, device_id=(li, peer(j)), device_id_type=MESH)
    sibling = (li + 1 - 2 * core, y)
    pl.semaphore_signal(barrier, inc=1, device_id=sibling, device_id_type=MESH)

    @pl.when(y != 0)
    def _():
        pl.semaphore_signal(barrier, inc=1, device_id=(partner(0), y), device_id_type=MESH)

    def sig(k, c):
        pl.semaphore_signal(barrier, inc=1, device_id=(partner(k), y), device_id_type=MESH)
        return c

    lax.fori_loop(1, nk, sig, 0)

    slab_copies = [pltpu.make_async_copy(slab_hbm.at[l], slab.at[l], slab_sem.at[l]) for l in range(2)]
    slab_copies.append(pltpu.make_async_copy(rowner_hbm, rowner_ref, slab_sem.at[2]))
    for c in slab_copies:
        c.start()

    nl = 2 * nk
    row = lax.broadcasted_iota(jnp.int32, (nl, q_ref.shape[0]), 0)
    kk = row % nk
    dz = kk // NC
    xd = x ^ y ^ (dz & 3)
    zd = z ^ dz
    cd = (core + kk) % NC
    lvec = ((xd * NZ + zd) * NC + cd) * 2 + row // nk
    hit = probes_ref[0:1, :] == lvec
    for j in range(1, 4):
        hit = hit | (probes_ref[j : j + 1, :] == lvec)
    hits = jnp.where(hit, 1.0, 0.0).astype(F32)
    qn = q_ref.shape[0]
    before = jnp.where(
        lax.broadcasted_iota(jnp.int32, (qn, qn), 0) < lax.broadcasted_iota(jnp.int32, (qn, qn), 1), 1.0, 0.0
    ).astype(BF16)
    rank = jnp.dot(hits.astype(BF16), before, preferred_element_type=F32)
    rank = jnp.where(hit, rank, -1.0)
    slot = lax.broadcasted_iota(jnp.int32, (CAP, qn), 0).astype(F32)
    for r in range(nl):
        onehot[r // nk, r % nk] = jnp.where(rank[r : r + 1, :] == slot, 1.0, 0.0).astype(BF16)
    def pick(l):
        picked = jnp.dot(onehot[l].reshape(nq, qn), q_ref[...], preferred_element_type=F32) * (1.0 / math.sqrt(feat))
        send_q[l] = picked.astype(BF16).reshape(nk, CAP, feat)

    pick(0)
    own8 = jnp.broadcast_to((owner_ref[...] + 1).astype(F32), (8, qn)).astype(BF16)
    for i in range(2):
        send_o[i : i + 1, :] = nt_dot(own8, onehot[i].reshape(nq, qn))[0:1, :]

    pl.semaphore_wait(barrier, 4 + nk - (1 - (y + 3) // 4))

    def q_copy(k, l):
        return pltpu.make_async_remote_copy(
            src_ref=send_q.at[l, k], dst_ref=recv_q.at[y, l, k], send_sem=a2a_s.at[l, k], recv_sem=a2a_r.at[l, k],
            device_id=(partner(k), y), device_id_type=MESH)

    def o_copy(k):
        return pltpu.make_async_remote_copy(
            src_ref=send_o, dst_ref=recv_o.at[k], send_sem=o_s.at[k], recv_sem=o_r.at[k],
            device_id=(partner(k), y), device_id_type=MESH)

    q_self = [pltpu.make_async_copy(send_q.at[l, 0], recv_q.at[y, l, 0], a2a_r.at[l, 0]) for l in range(2)]
    o_self = pltpu.make_async_copy(send_o, recv_o.at[0], o_r.at[0])

    def all_partners(alone, copy):
        @pl.when(y == 0)
        def _():
            alone()

        @pl.when(y != 0)
        def _():
            copy(0)

        def step(k, c):
            copy(nk - k)
            return c

        lax.fori_loop(1, nk, step, 0)

    all_partners(q_self[0].start, lambda k: q_copy(k, 0).start())
    all_partners(o_self.start, lambda k: o_copy(k).start())
    pick(1)
    all_partners(q_self[1].start, lambda k: q_copy(k, 1).start())
    bi[y] = jnp.broadcast_to(bias_ref[...].astype(F32).reshape(1, bias_ref.shape[0]), (8, bias_ref.shape[0]))

    ih, oh2 = 2 * feat // NC, wo.shape[1] // NC
    in_half = pl.ds(pl.multiple_of(core * ih, ih), ih)
    out_half = pl.ds(pl.multiple_of(core * oh2, oh2), oh2)

    def w_copies(j):
        return [
            pltpu.make_async_remote_copy(
                src_ref=s, dst_ref=d, send_sem=w_s.at[n, j - 1], recv_sem=w_r.at[n, j - 1],
                device_id=(li, peer(j)), device_id_type=MESH)
            for n, (s, d) in enumerate((
                (win_ref.at[in_half], wi.at[y, in_half]),
                (wout_ref.at[out_half], wo.at[y, out_half]),
                (bi.at[y], bi.at[y])))
        ]

    def share_copies(j):
        src = peer(NY - j)
        return [
            pltpu.make_async_remote_copy(
                src_ref=d, dst_ref=d, send_sem=f_s.at[n, j - 1], recv_sem=f_r.at[n, j - 1],
                device_id=sibling, device_id_type=MESH)
            for n, d in enumerate((wi.at[src, in_half], wo.at[src, out_half]))
        ]

    weight_copies = {j: w_copies(j) for j in (1, 3, 2)}
    for j in (1, 3, 2):
        for c in weight_copies[j][1:]:
            c.start()
    local = [pltpu.make_async_copy(win_ref, wi.at[y], loc_sem.at[0]), pltpu.make_async_copy(wout_ref, wo.at[y], loc_sem.at[1])]
    for c in local:
        c.start()

    onehot_t[...] = onehot[...].reshape(nl * CAP, qn).astype(F32).T.astype(BF16)
    kt[:, :, feat : feat + 16, :] = jnp.ones((2, ntile, 16, tile), BF16)
    ptile = min(tile, 512)
    slab_copies[2].wait()
    for l in range(2):
        slab_copies[l].wait()

        def prep(t, c):
            rows_t = slab[l, pl.ds(t * ptile, ptile), :]
            kt[l, t // (tile // ptile), 0:feat, pl.ds(t % (tile // ptile) * ptile, ptile)] = rows_t.astype(F32).T.astype(BF16)
            for h in range(ptile // 128):
                rr = rowner_ref[l : l + 1, pl.ds(t * ptile + h * 128, 128)].astype(F32)
                rcol[l, pl.ds(t * ptile + h * 128, 128), :] = jnp.broadcast_to(rr, (128, 128)).T
            return c

        lax.fori_loop(0, rows // ptile, prep, 0)

    half_of = (pl.ds(0, nk // 2), pl.ds(nk // 2, nk // 2))

    def near_copy(j, l):
        return pltpu.make_async_remote_copy(
            src_ref=recv_q.at[y, l], dst_ref=recv_q.at[y, l],
            send_sem=ag_s.at[j - 1, l, 0], recv_sem=ag_r.at[j - 1, l, 0],
            device_id=(li, peer(j)), device_id_type=MESH)

    def far_copy(p, l):
        src, dst = (peer(3), peer(1)) if p == 0 else (peer(1), peer(3))
        return pltpu.make_async_remote_copy(
            src_ref=recv_q.at[src, l, half_of[p]], dst_ref=recv_q.at[src, l, half_of[p]],
            send_sem=ag_s.at[1, l, p], recv_sem=ag_r.at[1, l, p],
            device_id=(li, dst), device_id_type=MESH)

    def owners_copy(j):
        return pltpu.make_async_remote_copy(
            src_ref=own_o.at[y], dst_ref=own_o.at[y], send_sem=ago_s.at[j - 1], recv_sem=ago_r.at[j - 1],
            device_id=(li, peer(j)), device_id_type=MESH)

    def gather(j, l):
        if j == 0:
            all_partners(q_self[l].wait, lambda k: q_copy(k, l).wait())
            for d in (1, 3):
                near_copy(d, l).start()
            if l == 0:
                all_partners(o_self.wait, lambda k: o_copy(k).wait())
                lane_k = lax.broadcasted_iota(jnp.int32, (2, nq), 1) // CAP
                total_o = jnp.zeros((2, nq), F32)
                for k in range(nk):
                    total_o = total_o + jnp.where(lane_k == k, recv_o[k], 0.0)
                own_o[y] = total_o - 1.0
                for d in (1, 3, 2):
                    owners_copy(d).start()
        elif j == 1:
            near_copy(1, l).wait_recv()
            far_copy(0, l).start()
            near_copy(3, l).wait_recv()
            far_copy(1, l).start()
        elif j == 2:
            far_copy(0, l).wait_recv()
            far_copy(1, l).wait_recv()
        if j != 0 and l == 0:
            owners_copy(j).wait_recv()

    order = [(0, 0), (0, 1), (1, 0), (3, 0), (1, 1), (2, 0), (3, 1), (2, 1)]
    rs_sends = []

    rows_of = (pl.ds(0, nq // 2), pl.ds(nq // 2, nq // 2))

    def rs_copy(j, l, p):
        return pltpu.make_async_remote_copy(
            src_ref=part.at[peer(j), l, rows_of[p]], dst_ref=rpart.at[j - 1, l, rows_of[p]],
            send_sem=rs_s.at[j - 1, l, p], recv_sem=rs_r.at[j - 1, l, p],
            device_id=(li, peer(j)), device_id_type=MESH)

    def rl_copy(j, l):
        return pltpu.make_async_remote_copy(
            src_ref=lse.at[peer(j), l], dst_ref=rlse.at[j - 1, l], send_sem=rl_s.at[j - 1, l],
            recv_sem=rl_r.at[j - 1, l], device_id=(li, peer(j)), device_id_type=MESH)

    def score_tile(n, l, t, own_row, m):
        s = jnp.dot(slab[l, pl.ds(t * tile, tile), :], qt[n % 2], preferred_element_type=F32)
        rc = rcol[l, pl.ds(t * tile, tile), :]
        halves = []
        for h in range(nq // 128):
            cols = slice(h * 128, (h + 1) * 128)
            sh = s[:, cols]
            sh = jnp.where(rc == own_row[:, cols], sh - SCORE_PEN, sh)
            scores[n % 2, t, :, cols] = sh
            halves.append(jnp.max(sh.reshape(tile // 8, 8, 128), axis=0))
        return jnp.maximum(m, jnp.concatenate(halves, axis=1))

    def sum_tile(n, l, t, peak):
        w = jnp.exp2(((scores[n % 2, t] - peak) * LOG2E).astype(BF16))
        acc[...] += jnp.dot(kt[l, t], w, preferred_element_type=F32)

    peak = None
    for n in range(len(order) + 1):
        own_row = None
        if n < len(order):
            j, l = order[n]
            src = peer(NY - j)
            gather(j, l)
            src = peer(NY - j)
            qt[n % 2] = recv_q[src, l].reshape(nq, feat).astype(F32).T.astype(BF16)
            own_row = own_o[src, l : l + 1, :]
        if n > 0:
            acc[...] = jnp.zeros_like(acc)
        prev_peak = peak

        def stage(t, m, n=n, own_row=own_row, prev_peak=prev_peak):
            if n > 0:
                sum_tile(n - 1, order[n - 1][1], t, prev_peak)
            if n < len(order):
                m = score_tile(n, order[n][1], t, own_row, m)
            return m

        m = lax.fori_loop(0, ntile, stage, jnp.full((8, nq), -jnp.inf, F32))
        if n > 0:
            pj, pl_ = order[n - 1]
            psrc = peer(NY - pj)
            total = acc[feat : feat + 1, :]
            mean = acc[0:feat, :] / total
            part[psrc, pl_] = mean.T.astype(BF16)
            lse[psrc, pl_] = prev_peak + jnp.log(total)
            if pj != 0:
                for c in (rl_copy(NY - pj, pl_), rs_copy(NY - pj, pl_, 1), rs_copy(NY - pj, pl_, 0)):
                    c.start()
                    rs_sends.append(c)
        if n < len(order):
            peak = jnp.max(m, axis=0, keepdims=True)

    for j in (1, 3, 2):
        weight_copies[j][0].start()

    def ret_copy(k, l):
        return pltpu.make_async_remote_copy(
            src_ref=ctx.at[l, k], dst_ref=ret.at[l, k], send_sem=ret_s.at[l, k], recv_sem=ret_r.at[l, k],
            device_id=(partner(k), y), device_id_type=MESH)

    def ret_self(l):
        return pltpu.make_async_copy(ctx.at[l, 0], ret.at[l, 0], ret_r.at[l, 0])

    def part_partners(p, alone, copy):
        if p == 0:

            @pl.when(y == 0)
            def _():
                alone()

            @pl.when(y != 0)
            def _():
                copy(0)

        first, last = max(1, p * nk // 2), (p + 1) * nk // 2

        def step(k, c):
            copy(first + last - 1 - k)
            return c

        lax.fori_loop(first, last, step, 0)

    for l in range(2):
        for j in (1, 3, 2):
            rl_copy(j, l).wait_recv()
        ls = [lse[y, l]] + [rlse[j - 1, l] for j in (1, 2, 3)]
        top = jnp.maximum(jnp.maximum(ls[0], ls[1]), jnp.maximum(ls[2], ls[3]))
        es = [jnp.exp(v - top) for v in ls]
        inv = 1.0 / (es[0] + es[1] + es[2] + es[3])
        cols = [jnp.broadcast_to(e * inv, (128, nq)).T for e in es]
        for p in (1, 0):
            for j in (1, 3, 2):
                rs_copy(j, l, p).wait_recv()
            rs = slice(p * nq // 2, (p + 1) * nq // 2)
            srcs = [part[y, l, rs]] + [rpart[j - 1, l, rs] for j in (1, 2, 3)]
            for h in range(feat // 128):
                cs = slice(h * 128, (h + 1) * 128)
                val = cols[0][rs] * srcs[0][:, cs].astype(F32)
                for a in range(1, 4):
                    val = val + cols[a][rs] * srcs[a][:, cs].astype(F32)
                ctx[l, p * nk // 2 : (p + 1) * nk // 2, :, cs] = val.astype(BF16).reshape(nk // 2, CAP, 128)
            part_partners(p, ret_self(l).start, lambda k, l=l: ret_copy(k, l).start())

    share = None
    for l in range(2):
        all_partners(ret_self(l).wait, lambda k, l=l: ret_copy(k, l).wait_recv())
        piece = jnp.dot(
            onehot_t[:, l * nq : (l + 1) * nq], ret[l].reshape(nq, feat), preferred_element_type=F32)
        share = piece if share is None else share + piece

    share = share * 0.25
    qb = qn // NY
    pq[...] = share.astype(BF16).reshape(NY, qb, feat)
    pq_copies = {}
    for j in (1, 2, 3):
        pq_copies[j] = pltpu.make_async_remote_copy(
            src_ref=pq.at[peer(j)], dst_ref=rpq.at[j - 1], send_sem=pq_s.at[j - 1], recv_sem=pq_r.at[j - 1],
            device_id=(li, peer(j)), device_id_type=MESH)
        pq_copies[j].start()
    for j in (1, 3, 2):
        for c in weight_copies[j]:
            c.wait()
        for c in share_copies(j):
            c.start()
    for j in (1, 3, 2):
        for c in share_copies(j):
            c.wait()
    for c in local:
        c.wait()
    mine = q_ref[pl.ds(pl.multiple_of(y * qb, qb), qb), :]
    hids = [jnp.dot(mine, wi[b, 0:feat, :], preferred_element_type=F32) + bi[b, 0:1, :] for b in range(NY)]
    for j in (1, 2, 3):
        pq_copies[j].wait()
    retrieved = pq[y].astype(F32)
    for j in (1, 2, 3):
        retrieved = retrieved + rpq[j - 1].astype(F32)
    normed = retrieved * lax.rsqrt(jnp.mean(retrieved * retrieved, axis=1, keepdims=True) + 1e-06)
    normed = normed.astype(BF16)
    res = jnp.zeros((qb, feat), F32)
    for b in range(NY):
        hid = hids[b] + jnp.dot(normed, wi[b, feat : 2 * feat, :], preferred_element_type=F32)
        hid = jax.nn.gelu(hid, approximate=True).astype(BF16)
        res = res + jnp.dot(hid, wo[b], preferred_element_type=F32)
    ob = feat // NY
    for b in range(NY):
        blk[b, :, 0:ob] = res[:, b * ob : (b + 1) * ob].astype(BF16)
        blk[b, :, ob:128] = jnp.zeros((qb, 128 - ob), BF16)
    blk_copies = {}
    for j in (1, 2, 3):
        blk_copies[j] = pltpu.make_async_remote_copy(
            src_ref=blk.at[peer(j)], dst_ref=rblk.at[y], send_sem=blk_s.at[j - 1], recv_sem=blk_r.at[j - 1],
            device_id=(li, peer(j)), device_id_type=MESH)
        blk_copies[j].start()
    rblk[y] = blk[y]
    for l in range(2):
        for j in (1, 3):
            near_copy(j, l).wait_send()
        for p in range(2):
            far_copy(p, l).wait_send()
    for j in (1, 2, 3):
        owners_copy(j).wait_send()
    for c in rs_sends:
        c.wait_send()
    for l in range(2):
        part_partners(1, None, lambda k, l=l: ret_copy(k, l).wait_send())

        @pl.when(y != 0)
        def _(l=l):
            ret_copy(0, l).wait_send()

        def ret_sent(k, c, l=l):
            ret_copy(k, l).wait_send()
            return c

        lax.fori_loop(1, nk // 2, ret_sent, 0)
    for j in (1, 2, 3):
        blk_copies[j].wait()
    full = rblk[...].reshape(qn, 128).astype(F32)
    out_ref[...] = full.T[0:ob, :].astype(BF16)


def body(queries, query_owner, probes, list_slab, row_owner, proj_in, bias_in, proj_out):
    qn, feat = queries.shape
    lists, rows = list_slab.shape[0], list_slab.shape[1]
    nk = NZ * NC
    nq = nk * CAP
    nl = 2 * nk
    tile = min(TILE, rows)
    nt = rows // tile
    hid = proj_in.shape[1]
    qb = qn // NY
    vm = pltpu.VMEM
    dma = pltpu.SemaphoreType.DMA
    vspec = pl.BlockSpec(memory_space=pltpu.VMEM)
    hbm = pl.BlockSpec(memory_space=pl.ANY)
    out_t = pl.pallas_call(
        kernel,
        out_shape=jax.ShapeDtypeStruct((feat // NY, qn), BF16),
        in_specs=[vspec, vspec, vspec, hbm, hbm, hbm, vspec, hbm],
        out_specs=vspec,
        scratch_shapes=[
            vm((lists, rows, feat), BF16),
            vm((lists, rows), jnp.int32),
            vm((lists, nt, feat + 16, tile), BF16),
            vm((lists, rows, 128), F32),
            vm((2, nk, CAP, qn), BF16),
            vm((qn, nl * CAP), BF16),
            vm((2, nk, CAP, feat), BF16),
            vm((2, nq), F32),
            vm((NY, 2, nk, CAP, feat), BF16),
            vm((nk, 2, nq), F32),
            vm((NY, 2, nq), F32),
            vm((2, feat, nq), BF16),
            vm((2, nt, tile, nq), F32),
            vm((feat + 16, nq), F32),
            vm((NY, 2, nq, feat), BF16),
            vm((NY, 2, 1, nq), F32),
            vm((NY - 1, 2, nq, feat), BF16),
            vm((NY - 1, 2, 1, nq), F32),
            vm((2, nk, CAP, feat), BF16),
            vm((2, nk, CAP, feat), BF16),
            vm((NY, qb, feat), BF16),
            vm((NY - 1, qb, feat), BF16),
            vm((NY, qb, 128), BF16),
            vm((NY, qb, 128), BF16),
            vm((NY, 2 * feat, hid), BF16),
            vm((NY, hid, feat), BF16),
            vm((NY, 8, hid), F32),
            dma((3,)),
            dma((2, nk)), dma((2, nk)), dma((nk,)), dma((nk,)),
            dma((3, 2, 2)), dma((3, 2, 2)), dma((3,)), dma((3,)),
            dma((3, 3)), dma((3, 3)),
            dma((3, 2, 2)), dma((3, 2, 2)), dma((3, 2)), dma((3, 2)),
            dma((2, 3)), dma((2, 3)), dma((2, nk)), dma((2, nk)),
            dma((3,)), dma((3,)), dma((3,)), dma((3,)),
            dma((2,)),
        ],
        compiler_params=pltpu.CompilerParams(
            collective_id=0, has_side_effects=True, vmem_limit_bytes=56 * 1024 * 1024
        ),
    )(queries, query_owner.reshape(1, qn), probes.T, list_slab, row_owner, proj_in, bias_in, proj_out)
    return out_t.T


def solution(mesh):
    in_specs = (
        P("list", None),
        P("list"),
        P("list", None),
        P("list", "row", None),
        P("list", "row"),
        P(None, "row"),
        P("row"),
        P("row", None),
    )
    out_specs = P("list", "row")
    return jax.shard_map(body, mesh=mesh, in_specs=in_specs, out_specs=out_specs, check_vma=False)
```

```python
import math

import jax
import jax.numpy as jnp
from jax import lax
from jax.experimental import pallas as pl
from jax.experimental.pallas import tpu as pltpu
from jax.sharding import PartitionSpec as P

SCORE_PEN = 10000.0
LOG2E = math.log2(math.e)
NX, NZ, NC, NY = 4, 8, 2, 4
CAP = 16
TILE = 2048
MESH = pl.DeviceIdType.MESH
F32 = jnp.float32
BF16 = jnp.bfloat16


def xor(a, b, bits):
    out = 0
    for i in range(bits):
        out = out + ((a // 2**i + b // 2**i) % 2) * 2**i
    return out


def nt_dot(a, b):
    return lax.dot_general(a, b, (((1,), (1,)), ((), ())), preferred_element_type=F32)


def kernel(
    q_ref, owner_ref, probes_ref, slab_hbm, rowner_hbm, win_ref, bias_ref, wout_ref,
    out_ref,
    slab, rowner_ref, kt, rcol, onehot, onehot_t, send_q, send_o, recv_q, recv_o, own_o, qt, scores, acc,
    part, lse, rpart, rlse, ctx, ret, pq, rpq, blk, rblk, wi, wo, bi,
    slab_sem, a2a_s, a2a_r, o_s, o_r, ag_s, ag_r, ago_s, ago_r, w_s, w_r, rs_s, rs_r, rl_s, rl_r,
    f_s, f_r, ret_s, ret_r, pq_s, pq_r, blk_s, blk_r, loc_sem,
):
    nk = NZ * NC
    nq = nk * CAP
    rows = slab.shape[1]
    feat = slab.shape[2]
    tile = scores.shape[2]
    ntile = rows // tile
    li = lax.axis_index("list")
    y = lax.axis_index("row")
    core = li % NC
    z = (li // NC) % NZ
    x = li // (NC * NZ)

    def partner(k):
        dz, dc = k // NC, k % NC
        return (xor(x, xor(y, dz % 4, 2), 2) * NZ + xor(z, dz, 3)) * NC + (core + dc) % NC

    def peer(j):
        return (y + j) % NY

    barrier = pltpu.get_barrier_semaphore()
    for j in (1, 2, 3):
        pl.semaphore_signal(barrier, inc=1, device_id=(li, peer(j)), device_id_type=MESH)
    sibling = (li + 1 - 2 * core, y)
    pl.semaphore_signal(barrier, inc=1, device_id=sibling, device_id_type=MESH)

    @pl.when(y != 0)
    def _():
        pl.semaphore_signal(barrier, inc=1, device_id=(partner(0), y), device_id_type=MESH)

    def sig(k, c):
        pl.semaphore_signal(barrier, inc=1, device_id=(partner(k), y), device_id_type=MESH)
        return c

    lax.fori_loop(1, nk, sig, 0)

    slab_copies = [pltpu.make_async_copy(slab_hbm.at[l], slab.at[l], slab_sem.at[l]) for l in range(2)]
    slab_copies.append(pltpu.make_async_copy(rowner_hbm, rowner_ref, slab_sem.at[2]))
    for c in slab_copies:
        c.start()

    nl = 2 * nk
    row = lax.broadcasted_iota(jnp.int32, (nl, q_ref.shape[0]), 0)
    kk = row % nk
    dz = kk // NC
    xd = x ^ y ^ (dz & 3)
    zd = z ^ dz
    cd = (core + kk) % NC
    lvec = ((xd * NZ + zd) * NC + cd) * 2 + row // nk
    hit = probes_ref[0:1, :] == lvec
    for j in range(1, 4):
        hit = hit | (probes_ref[j : j + 1, :] == lvec)
    hits = jnp.where(hit, 1.0, 0.0).astype(F32)
    qn = q_ref.shape[0]
    before = jnp.where(
        lax.broadcasted_iota(jnp.int32, (qn, qn), 0) < lax.broadcasted_iota(jnp.int32, (qn, qn), 1), 1.0, 0.0
    ).astype(BF16)
    rank = jnp.dot(hits.astype(BF16), before, preferred_element_type=F32)
    rank = jnp.where(hit, rank, -1.0)
    slot = lax.broadcasted_iota(jnp.int32, (CAP, qn), 0).astype(F32)
    for r in range(nl):
        onehot[r // nk, r % nk] = jnp.where(rank[r : r + 1, :] == slot, 1.0, 0.0).astype(BF16)
    def pick(l):
        picked = jnp.dot(onehot[l].reshape(nq, qn), q_ref[...], preferred_element_type=F32) * (1.0 / math.sqrt(feat))
        send_q[l] = picked.astype(BF16).reshape(nk, CAP, feat)

    pick(0)
    own8 = jnp.broadcast_to((owner_ref[...] + 1).astype(F32), (8, qn)).astype(BF16)
    for i in range(2):
        send_o[i : i + 1, :] = nt_dot(own8, onehot[i].reshape(nq, qn))[0:1, :]

    pl.semaphore_wait(barrier, 4 + nk - (1 - (y + 3) // 4))

    def q_copy(k, l):
        return pltpu.make_async_remote_copy(
            src_ref=send_q.at[l, k], dst_ref=recv_q.at[y, l, k], send_sem=a2a_s.at[l, k], recv_sem=a2a_r.at[l, k],
            device_id=(partner(k), y), device_id_type=MESH)

    def o_copy(k):
        return pltpu.make_async_remote_copy(
            src_ref=send_o, dst_ref=recv_o.at[k], send_sem=o_s.at[k], recv_sem=o_r.at[k],
            device_id=(partner(k), y), device_id_type=MESH)

    q_self = [pltpu.make_async_copy(send_q.at[l, 0], recv_q.at[y, l, 0], a2a_r.at[l, 0]) for l in range(2)]
    o_self = pltpu.make_async_copy(send_o, recv_o.at[0], o_r.at[0])

    def all_partners(alone, copy):
        @pl.when(y == 0)
        def _():
            alone()

        @pl.when(y != 0)
        def _():
            copy(0)

        def step(k, c):
            copy(nk - k)
            return c

        lax.fori_loop(1, nk, step, 0)

    all_partners(q_self[0].start, lambda k: q_copy(k, 0).start())
    all_partners(o_self.start, lambda k: o_copy(k).start())
    pick(1)
    all_partners(q_self[1].start, lambda k: q_copy(k, 1).start())
    bi[y] = jnp.broadcast_to(bias_ref[...].astype(F32).reshape(1, bias_ref.shape[0]), (8, bias_ref.shape[0]))

    ih, oh2 = 2 * feat // NC, wo.shape[1] // NC
    in_half = pl.ds(pl.multiple_of(core * ih, ih), ih)
    out_half = pl.ds(pl.multiple_of(core * oh2, oh2), oh2)

    def w_copies(j):
        return [
            pltpu.make_async_remote_copy(
                src_ref=s, dst_ref=d, send_sem=w_s.at[n, j - 1], recv_sem=w_r.at[n, j - 1],
                device_id=(li, peer(j)), device_id_type=MESH)
            for n, (s, d) in enumerate((
                (win_ref.at[in_half], wi.at[y, in_half]),
                (wout_ref.at[out_half], wo.at[y, out_half]),
                (bi.at[y], bi.at[y])))
        ]

    def share_copies(j):
        src = peer(NY - j)
        return [
            pltpu.make_async_remote_copy(
                src_ref=d, dst_ref=d, send_sem=f_s.at[n, j - 1], recv_sem=f_r.at[n, j - 1],
                device_id=sibling, device_id_type=MESH)
            for n, d in enumerate((wi.at[src, in_half], wo.at[src, out_half]))
        ]

    weight_copies = {j: w_copies(j) for j in (1, 3, 2)}
    for j in (1, 3, 2):
        for c in weight_copies[j][1:]:
            c.start()
    local = [pltpu.make_async_copy(win_ref, wi.at[y], loc_sem.at[0]), pltpu.make_async_copy(wout_ref, wo.at[y], loc_sem.at[1])]
    for c in local:
        c.start()

    onehot_t[...] = onehot[...].reshape(nl * CAP, qn).astype(F32).T.astype(BF16)
    kt[:, :, feat : feat + 16, :] = jnp.ones((2, ntile, 16, tile), BF16)
    ptile = min(tile, 512)
    slab_copies[2].wait()
    for l in range(2):
        slab_copies[l].wait()

        def prep(t, c):
            rows_t = slab[l, pl.ds(t * ptile, ptile), :]
            kt[l, t // (tile // ptile), 0:feat, pl.ds(t % (tile // ptile) * ptile, ptile)] = rows_t.astype(F32).T.astype(BF16)
            for h in range(ptile // 128):
                rr = rowner_ref[l : l + 1, pl.ds(t * ptile + h * 128, 128)].astype(F32)
                rcol[l, pl.ds(t * ptile + h * 128, 128), :] = jnp.broadcast_to(rr, (128, 128)).T
            return c

        lax.fori_loop(0, rows // ptile, prep, 0)

    half_of = (pl.ds(0, nk // 2), pl.ds(nk // 2, nk // 2))

    def near_copy(j, l):
        return pltpu.make_async_remote_copy(
            src_ref=recv_q.at[y, l], dst_ref=recv_q.at[y, l],
            send_sem=ag_s.at[j - 1, l, 0], recv_sem=ag_r.at[j - 1, l, 0],
            device_id=(li, peer(j)), device_id_type=MESH)

    def far_copy(p, l):
        src, dst = (peer(3), peer(1)) if p == 0 else (peer(1), peer(3))
        return pltpu.make_async_remote_copy(
            src_ref=recv_q.at[src, l, half_of[p]], dst_ref=recv_q.at[src, l, half_of[p]],
            send_sem=ag_s.at[1, l, p], recv_sem=ag_r.at[1, l, p],
            device_id=(li, dst), device_id_type=MESH)

    def owners_copy(j):
        return pltpu.make_async_remote_copy(
            src_ref=own_o.at[y], dst_ref=own_o.at[y], send_sem=ago_s.at[j - 1], recv_sem=ago_r.at[j - 1],
            device_id=(li, peer(j)), device_id_type=MESH)

    def gather(j, l):
        if j == 0:
            all_partners(q_self[l].wait, lambda k: q_copy(k, l).wait())
            for d in (1, 3):
                near_copy(d, l).start()
            if l == 0:
                all_partners(o_self.wait, lambda k: o_copy(k).wait())
                lane_k = lax.broadcasted_iota(jnp.int32, (2, nq), 1) // CAP
                total_o = jnp.zeros((2, nq), F32)
                for k in range(nk):
                    total_o = total_o + jnp.where(lane_k == k, recv_o[k], 0.0)
                own_o[y] = total_o - 1.0
                for d in (1, 3, 2):
                    owners_copy(d).start()
        elif j == 1:
            near_copy(1, l).wait_recv()
            far_copy(0, l).start()
            near_copy(3, l).wait_recv()
            far_copy(1, l).start()
        elif j == 2:
            far_copy(0, l).wait_recv()
            far_copy(1, l).wait_recv()
        if j != 0 and l == 0:
            owners_copy(j).wait_recv()

    order = [(0, 0), (0, 1), (1, 0), (3, 0), (1, 1), (2, 0), (3, 1), (2, 1)]
    rs_sends = []

    rows_of = (pl.ds(0, nq // 2), pl.ds(nq // 2, nq // 2))

    def rs_copy(j, l, p):
        return pltpu.make_async_remote_copy(
            src_ref=part.at[peer(j), l, rows_of[p]], dst_ref=rpart.at[j - 1, l, rows_of[p]],
            send_sem=rs_s.at[j - 1, l, p], recv_sem=rs_r.at[j - 1, l, p],
            device_id=(li, peer(j)), device_id_type=MESH)

    def rl_copy(j, l):
        return pltpu.make_async_remote_copy(
            src_ref=lse.at[peer(j), l], dst_ref=rlse.at[j - 1, l], send_sem=rl_s.at[j - 1, l],
            recv_sem=rl_r.at[j - 1, l], device_id=(li, peer(j)), device_id_type=MESH)

    def score_tile(n, l, t, own_row, m):
        s = jnp.dot(slab[l, pl.ds(t * tile, tile), :], qt[n % 2], preferred_element_type=F32)
        rc = rcol[l, pl.ds(t * tile, tile), :]
        halves = []
        for h in range(nq // 128):
            cols = slice(h * 128, (h + 1) * 128)
            sh = s[:, cols]
            sh = jnp.where(rc == own_row[:, cols], sh - SCORE_PEN, sh)
            scores[n % 2, t, :, cols] = sh
            halves.append(jnp.max(sh.reshape(tile // 8, 8, 128), axis=0))
        return jnp.maximum(m, jnp.concatenate(halves, axis=1))

    def sum_tile(n, l, t, peak):
        w = jnp.exp2(((scores[n % 2, t] - peak) * LOG2E).astype(BF16))
        acc[...] += jnp.dot(kt[l, t], w, preferred_element_type=F32)

    peak = None
    for n in range(len(order) + 1):
        own_row = None
        if n < len(order):
            j, l = order[n]
            src = peer(NY - j)
            gather(j, l)
            src = peer(NY - j)
            qt[n % 2] = recv_q[src, l].reshape(nq, feat).astype(F32).T.astype(BF16)
            own_row = own_o[src, l : l + 1, :]
        if n > 0:
            acc[...] = jnp.zeros_like(acc)
        prev_peak = peak

        def stage(t, m, n=n, own_row=own_row, prev_peak=prev_peak):
            if n > 0:
                sum_tile(n - 1, order[n - 1][1], t, prev_peak)
            if n < len(order):
                m = score_tile(n, order[n][1], t, own_row, m)
            return m

        m = lax.fori_loop(0, ntile, stage, jnp.full((8, nq), -jnp.inf, F32))
        if n > 0:
            pj, pl_ = order[n - 1]
            psrc = peer(NY - pj)
            total = acc[feat : feat + 1, :]
            mean = acc[0:feat, :] / total
            part[psrc, pl_] = mean.T.astype(BF16)
            lse[psrc, pl_] = prev_peak + jnp.log(total)
            if pj != 0:
                for c in (rl_copy(NY - pj, pl_), rs_copy(NY - pj, pl_, 1), rs_copy(NY - pj, pl_, 0)):
                    c.start()
                    rs_sends.append(c)
        if n < len(order):
            peak = jnp.max(m, axis=0, keepdims=True)


    def ret_copy(k, l):
        return pltpu.make_async_remote_copy(
            src_ref=ctx.at[l, k], dst_ref=ret.at[l, k], send_sem=ret_s.at[l, k], recv_sem=ret_r.at[l, k],
            device_id=(partner(k), y), device_id_type=MESH)

    def ret_self(l):
        return pltpu.make_async_copy(ctx.at[l, 0], ret.at[l, 0], ret_r.at[l, 0])

    def part_partners(p, alone, copy):
        if p == 0:

            @pl.when(y == 0)
            def _():
                alone()

            @pl.when(y != 0)
            def _():
                copy(0)

        first, last = max(1, p * nk // 2), (p + 1) * nk // 2

        def step(k, c):
            copy(first + last - 1 - k)
            return c

        lax.fori_loop(first, last, step, 0)

    for l in range(2):
        for j in (1, 3, 2):
            rl_copy(j, l).wait_recv()
        ls = [lse[y, l]] + [rlse[j - 1, l] for j in (1, 2, 3)]
        top = jnp.maximum(jnp.maximum(ls[0], ls[1]), jnp.maximum(ls[2], ls[3]))
        es = [jnp.exp(v - top) for v in ls]
        inv = 1.0 / (es[0] + es[1] + es[2] + es[3])
        cols = [jnp.broadcast_to(e * inv, (128, nq)).T for e in es]
        for p in (1, 0):
            for j in (1, 3, 2):
                rs_copy(j, l, p).wait_recv()
            rs = slice(p * nq // 2, (p + 1) * nq // 2)
            srcs = [part[y, l, rs]] + [rpart[j - 1, l, rs] for j in (1, 2, 3)]
            for h in range(feat // 128):
                cs = slice(h * 128, (h + 1) * 128)
                val = cols[0][rs] * srcs[0][:, cs].astype(F32)
                for a in range(1, 4):
                    val = val + cols[a][rs] * srcs[a][:, cs].astype(F32)
                ctx[l, p * nk // 2 : (p + 1) * nk // 2, :, cs] = val.astype(BF16).reshape(nk // 2, CAP, 128)
            part_partners(p, ret_self(l).start, lambda k, l=l: ret_copy(k, l).start())
        if l == 0:
            for j in (1, 3, 2):
                weight_copies[j][0].start()

    share = None
    for l in range(2):
        all_partners(ret_self(l).wait, lambda k, l=l: ret_copy(k, l).wait_recv())
        piece = jnp.dot(
            onehot_t[:, l * nq : (l + 1) * nq], ret[l].reshape(nq, feat), preferred_element_type=F32)
        share = piece if share is None else share + piece

    share = share * 0.25
    qb = qn // NY
    pq[...] = share.astype(BF16).reshape(NY, qb, feat)
    pq_copies = {}
    for j in (1, 2, 3):
        pq_copies[j] = pltpu.make_async_remote_copy(
            src_ref=pq.at[peer(j)], dst_ref=rpq.at[j - 1], send_sem=pq_s.at[j - 1], recv_sem=pq_r.at[j - 1],
            device_id=(li, peer(j)), device_id_type=MESH)
        pq_copies[j].start()
    for j in (1, 3, 2):
        for c in weight_copies[j]:
            c.wait()
        for c in share_copies(j):
            c.start()
    for j in (1, 3, 2):
        for c in share_copies(j):
            c.wait()
    for c in local:
        c.wait()
    mine = q_ref[pl.ds(pl.multiple_of(y * qb, qb), qb), :]
    hids = [jnp.dot(mine, wi[b, 0:feat, :], preferred_element_type=F32) + bi[b, 0:1, :] for b in range(NY)]
    for j in (1, 2, 3):
        pq_copies[j].wait()
    retrieved = pq[y].astype(F32)
    for j in (1, 2, 3):
        retrieved = retrieved + rpq[j - 1].astype(F32)
    normed = retrieved * lax.rsqrt(jnp.mean(retrieved * retrieved, axis=1, keepdims=True) + 1e-06)
    normed = normed.astype(BF16)
    res = jnp.zeros((qb, feat), F32)
    for b in range(NY):
        hid = hids[b] + jnp.dot(normed, wi[b, feat : 2 * feat, :], preferred_element_type=F32)
        hid = jax.nn.gelu(hid, approximate=True).astype(BF16)
        res = res + jnp.dot(hid, wo[b], preferred_element_type=F32)
    ob = feat // NY
    for b in range(NY):
        blk[b, :, 0:ob] = res[:, b * ob : (b + 1) * ob].astype(BF16)
        blk[b, :, ob:128] = jnp.zeros((qb, 128 - ob), BF16)
    blk_copies = {}
    for j in (1, 2, 3):
        blk_copies[j] = pltpu.make_async_remote_copy(
            src_ref=blk.at[peer(j)], dst_ref=rblk.at[y], send_sem=blk_s.at[j - 1], recv_sem=blk_r.at[j - 1],
            device_id=(li, peer(j)), device_id_type=MESH)
        blk_copies[j].start()
    rblk[y] = blk[y]
    for l in range(2):
        for j in (1, 3):
            near_copy(j, l).wait_send()
        for p in range(2):
            far_copy(p, l).wait_send()
    for j in (1, 2, 3):
        owners_copy(j).wait_send()
    for c in rs_sends:
        c.wait_send()
    for l in range(2):
        part_partners(1, None, lambda k, l=l: ret_copy(k, l).wait_send())

        @pl.when(y != 0)
        def _(l=l):
            ret_copy(0, l).wait_send()

        def ret_sent(k, c, l=l):
            ret_copy(k, l).wait_send()
            return c

        lax.fori_loop(1, nk // 2, ret_sent, 0)
    for j in (1, 2, 3):
        blk_copies[j].wait()
    full = rblk[...].reshape(qn, 128).astype(F32)
    out_ref[...] = full.T[0:ob, :].astype(BF16)


def body(queries, query_owner, probes, list_slab, row_owner, proj_in, bias_in, proj_out):
    qn, feat = queries.shape
    lists, rows = list_slab.shape[0], list_slab.shape[1]
    nk = NZ * NC
    nq = nk * CAP
    nl = 2 * nk
    tile = min(TILE, rows)
    nt = rows // tile
    hid = proj_in.shape[1]
    qb = qn // NY
    vm = pltpu.VMEM
    dma = pltpu.SemaphoreType.DMA
    vspec = pl.BlockSpec(memory_space=pltpu.VMEM)
    hbm = pl.BlockSpec(memory_space=pl.ANY)
    out_t = pl.pallas_call(
        kernel,
        out_shape=jax.ShapeDtypeStruct((feat // NY, qn), BF16),
        in_specs=[vspec, vspec, vspec, hbm, hbm, hbm, vspec, hbm],
        out_specs=vspec,
        scratch_shapes=[
            vm((lists, rows, feat), BF16),
            vm((lists, rows), jnp.int32),
            vm((lists, nt, feat + 16, tile), BF16),
            vm((lists, rows, 128), F32),
            vm((2, nk, CAP, qn), BF16),
            vm((qn, nl * CAP), BF16),
            vm((2, nk, CAP, feat), BF16),
            vm((2, nq), F32),
            vm((NY, 2, nk, CAP, feat), BF16),
            vm((nk, 2, nq), F32),
            vm((NY, 2, nq), F32),
            vm((2, feat, nq), BF16),
            vm((2, nt, tile, nq), F32),
            vm((feat + 16, nq), F32),
            vm((NY, 2, nq, feat), BF16),
            vm((NY, 2, 1, nq), F32),
            vm((NY - 1, 2, nq, feat), BF16),
            vm((NY - 1, 2, 1, nq), F32),
            vm((2, nk, CAP, feat), BF16),
            vm((2, nk, CAP, feat), BF16),
            vm((NY, qb, feat), BF16),
            vm((NY - 1, qb, feat), BF16),
            vm((NY, qb, 128), BF16),
            vm((NY, qb, 128), BF16),
            vm((NY, 2 * feat, hid), BF16),
            vm((NY, hid, feat), BF16),
            vm((NY, 8, hid), F32),
            dma((3,)),
            dma((2, nk)), dma((2, nk)), dma((nk,)), dma((nk,)),
            dma((3, 2, 2)), dma((3, 2, 2)), dma((3,)), dma((3,)),
            dma((3, 3)), dma((3, 3)),
            dma((3, 2, 2)), dma((3, 2, 2)), dma((3, 2)), dma((3, 2)),
            dma((2, 3)), dma((2, 3)), dma((2, nk)), dma((2, nk)),
            dma((3,)), dma((3,)), dma((3,)), dma((3,)),
            dma((2,)),
        ],
        compiler_params=pltpu.CompilerParams(
            collective_id=0, has_side_effects=True, vmem_limit_bytes=56 * 1024 * 1024
        ),
    )(queries, query_owner.reshape(1, qn), probes.T, list_slab, row_owner, proj_in, bias_in, proj_out)
    return out_t.T


def solution(mesh):
    in_specs = (
        P("list", None),
        P("list"),
        P("list", None),
        P("list", "row", None),
        P("list", "row"),
        P(None, "row"),
        P("row"),
        P("row", None),
    )
    out_specs = P("list", "row")
    return jax.shard_map(body, mesh=mesh, in_specs=in_specs, out_specs=out_specs, check_vma=False)
```
